32 devices in a mesh: dp: 16 (over z, y, core), mp: 2 (over x).
Axes of the slice: x: 2, y: 2, z: 4, core: 2. Of those that a mesh axis runs over, the one named last changes fastest.
Arguments:
- activations: bfloat16 [16384, 4096], P('dp', 'mp'), may hold values from -6 to 6
- out_grad: bfloat16 [16384, 14336], P('dp', 'mp'), may hold values from -0.046875 to 0.046875
- tile_list: int32 [2, 16, 2], P('mp'), may hold values from 0 to 111, as said below
- tile_count: int32 [2], P('mp'), may hold values from 8 to 16, as said below
Outputs:
- grad_tiles: float32 [2, 16, 128, 128], P('mp', 'dp')
The draws below stay inside these ranges and needn't reach their ends.
Inputs may be any that keep to these rules, and one draw needn't show every extreme that they name: `tile_list`: in shard c the 16 entries name distinct blocks; the block row lies in 0 to 31 and the block column in c * 56 to (c + 1) * 56 - 1. `tile_count`: some shard has all 16 slots live.
All inputs are finite; a program needn't handle non-finite values.
Results may differ from the reference program's by a relative error of at most 0.0003.
Values may be sent and summed in bfloat16 or wider, within the bound.
No kernel may reach another device: no remote copies, remote signals or barrier semaphores. Data moves between devices by JAX's collectives and lax.ppermute only.
A program may use at most 128 MiB of HBM per device.

```python
import jax
import jax.numpy as jnp
from jax import lax

D = 4096
FF = 14336
BLK = 128
SLOTS = 1
TOKENS = 16384
N_DP = 16
N_MP = 2


def draw_tile_list(key, part):
    per_shard = FF // (N_MP * BLK)
    block_total = D // BLK * per_shard
    slot_total = N_DP * SLOTS

    def one_shard(shard_id):
        shuffled = jax.random.permutation(jax.random.fold_in(key, shard_id), block_total)[:slot_total]
        return jnp.stack([shuffled // per_shard, shard_id * per_shard + shuffled % per_shard], axis=-1)
    return jax.vmap(one_shard)(jnp.arange(N_MP, dtype=jnp.int32)).astype(jnp.int32)


def draw_tile_count(key, part):
    slot_total = N_DP * SLOTS
    lowest = slot_total // 2
    counts = jax.random.randint(jax.random.fold_in(key, 11), (N_MP,), lowest, slot_total + 1)
    fullest = jax.random.randint(jax.random.fold_in(key, 12), (), 0, N_MP)
    positions = jnp.arange(N_MP, dtype=jnp.int32)
    counts = jnp.where(positions == fullest, slot_total, counts)
    counts = jnp.where(positions == (fullest + 1) % N_MP, lowest, counts)
    return counts.astype(jnp.int32)


def level_of(rng, shape, cuts, low, high):
    loudness = 1.0
    for axis_at, shards_of in cuts:
        heights = jax.random.uniform(jax.random.fold_in(jax.random.fold_in(rng, 6), axis_at), (shards_of,), jnp.float32, low / len(cuts), high / len(cuts))
        loudness = loudness * jnp.repeat(jnp.exp(heights), shape[axis_at] // shards_of).reshape((-1,) + (1,) * (len(shape) - 1 - axis_at))
    return loudness


def normal_values(key, extent, spread, reach, split=(), held_as=jnp.bfloat16):
    values = spread * jax.random.normal(key, extent, jnp.float32)
    if split:
        values = values * level_of(key, extent, split, -0.22, 0.18)
    return jnp.clip(values, -reach, reach).astype(held_as)


def setup_inputs(seed: int = 0) -> dict:
    splits = jax.random.split(jax.random.key(seed), 5)
    return {
        "activations": normal_values(splits[0], (TOKENS, D), 1.0, 6.0, ((0, 16), (1, 2))),
        "out_grad": normal_values(splits[1], (TOKENS, FF), (1.0 / TOKENS ** 0.5), 0.046875, ((0, 16), (1, 2))),
        "tile_list": draw_tile_list(jax.random.fold_in(splits[4], 71), 0),
        "tile_count": draw_tile_count(jax.random.fold_in(splits[4], 71), 0),
    }


def reference(activations, out_grad, tile_list, tile_count):
    slot_total = tile_list.shape[1]
    flat_list = tile_list.reshape(-1, 2).astype(jnp.int32)
    shard_ids = jnp.repeat(jnp.arange(N_MP, dtype=jnp.int32), slot_total)
    slot_ids = jnp.tile(jnp.arange(slot_total, dtype=jnp.int32), N_MP)

    def tile_product(entry):
        row_block, col_block, shard_id, slot_id = entry
        act_cols = lax.dynamic_slice_in_dim(activations, (row_block * BLK).astype(jnp.int32), BLK, 1)
        grad_cols = lax.dynamic_slice_in_dim(out_grad, (col_block * BLK).astype(jnp.int32), BLK, 1)
        product = jnp.dot(act_cols.T, grad_cols, preferred_element_type=jnp.float32)
        return jnp.where(slot_id < tile_count[shard_id], product, jnp.zeros_like(product))

    products = lax.map(tile_product, (flat_list[:, 0], flat_list[:, 1], shard_ids, slot_ids))
    return products.reshape(N_MP, slot_total, BLK, BLK)
```

```python
import functools

import jax
import jax.numpy as jnp
from jax import lax
from jax.experimental import pallas as pl
from jax.experimental.pallas import tpu as pltpu
from jax.sharding import PartitionSpec as P

BLK = 128
VMEM_BYTES = 40 * 1024 * 1024


def pack_kernel(wanted_ref, act_ref, out_ref, sems):
    blocks = wanted_ref.shape[0]
    place = jnp.int32(0)
    copies = []
    for b in range(blocks):
        wanted = wanted_ref[b] > 0
        copy = pltpu.make_async_copy(
            act_ref.at[:, pl.ds(b * BLK, BLK)],
            out_ref.at[jnp.minimum(place, out_ref.shape[0] - 1)],
            sems.at[b],
        )
        pl.when(wanted)(copy.start)
        copies.append((wanted, copy))
        place = place + wanted.astype(jnp.int32)
    for wanted, copy in copies:
        pl.when(wanted)(copy.wait)


def pack(wanted, activations, count):
    tokens = activations.shape[0]
    return pl.pallas_call(
        pack_kernel,
        out_shape=jax.ShapeDtypeStruct((count, tokens, BLK), activations.dtype),
        in_specs=[pl.BlockSpec(memory_space=pltpu.SMEM), pl.BlockSpec(memory_space=pl.ANY)],
        out_specs=pl.BlockSpec(memory_space=pl.ANY),
        scratch_shapes=[pltpu.SemaphoreType.DMA((wanted.shape[0],))],
        cost_estimate=pl.CostEstimate(
            flops=0, bytes_accessed=count * tokens * BLK * 4, transcendentals=0
        ),
        name="pack",
    )(wanted, activations)


def tiles_kernel(order, by_block, fresh, plan_ref, rows_ref, grad_ref, *rest):
    if fresh:
        out_refs, (row_buf, grad_buf, row_sems, grad_sems) = rest[:2], rest[2:]
    else:
        out_refs, (row_buf, grad_buf, row_sems, grad_sems, stage, out_sems) = rest[2:4], rest[4:]
    me = lax.axis_index("dp")
    half = out_refs[0].shape[0]
    per_owner = plan_ref.shape[1] // len(order)
    depth = row_buf.shape[0]
    jobs = []
    for place, relative in enumerate(order):
        for lane in range(per_owner):
            slot = (me ^ relative) * per_owner + lane
            jobs.append((slot, place * per_owner + lane))

    def loads(n):
        slot, _ = jobs[n]
        block = jnp.maximum(plan_ref[0, slot], 0)
        column = plan_ref[1, slot]
        if by_block:
            source = rows_ref.at[jnp.minimum(block, rows_ref.shape[0] - 1)]
        else:
            source = rows_ref.at[:, pl.ds(pl.multiple_of(block * BLK, BLK), BLK)]
        at = n % depth
        return (
            plan_ref[0, slot] >= 0,
            pltpu.make_async_copy(source, row_buf.at[at], row_sems.at[at]),
            pltpu.make_async_copy(
                grad_ref.at[:, pl.ds(pl.multiple_of(column * BLK, BLK), BLK)],
                grad_buf.at[at],
                grad_sems.at[at],
            ),
        )

    def start(n):
        used, row_copy, grad_copy = loads(n)

        @pl.when(used)
        def _():
            row_copy.start()
            grad_copy.start()

    def out_copy(n):
        place = jobs[n][1]
        return pltpu.make_async_copy(
            stage.at[n], out_refs[place // half].at[place % half], out_sems.at[n]
        )

    for n in range(min(depth, len(jobs))):
        start(n)
    for n in range(len(jobs)):
        used, row_copy, grad_copy = loads(n)
        place = jobs[n][1]

        @pl.when(used)
        def _():
            row_copy.wait()
            grad_copy.wait()
            product = lax.dot_general(
                row_buf[n % depth],
                grad_buf[n % depth],
                (((0,), (0,)), ((), ())),
                preferred_element_type=jnp.float32,
            )
            if fresh:
                out_refs[place // half][place % half] = product
            else:
                stage[n] = product
                out_copy(n).start()

        if fresh:

            @pl.when(jnp.logical_not(used))
            def _():
                out_refs[place // half][place % half] = jnp.zeros((BLK, BLK), jnp.float32)

        if n + depth < len(jobs):
            start(n + depth)
    if not fresh:
        for n in range(len(jobs)):
            pl.when(plan_ref[0, jobs[n][0]] >= 0)(out_copy(n).wait)


def tiles(order, plan, rows, out_grad, partial=None):
    fresh = partial is None
    by_block = rows.ndim == 3
    tokens = out_grad.shape[0]
    slots = plan.shape[1]
    depth = min(slots, 16)
    half = jax.ShapeDtypeStruct((slots // 2, BLK, BLK), jnp.float32)
    anywhere = pl.BlockSpec(memory_space=pl.ANY)
    scratch = [
        pltpu.VMEM((depth, tokens, BLK), rows.dtype),
        pltpu.VMEM((depth, tokens, BLK), out_grad.dtype),
        pltpu.SemaphoreType.DMA((depth,)),
        pltpu.SemaphoreType.DMA((depth,)),
    ]
    if not fresh:
        scratch += [pltpu.VMEM((slots, BLK, BLK), jnp.float32), pltpu.SemaphoreType.DMA((slots,))]
    return pl.pallas_call(
        functools.partial(tiles_kernel, order, by_block, fresh),
        out_shape=(half, half),
        in_specs=[pl.BlockSpec(memory_space=pltpu.SMEM), anywhere, anywhere]
        + ([] if fresh else [anywhere, anywhere]),
        out_specs=(pl.BlockSpec(memory_space=pltpu.VMEM),) * 2 if fresh else (anywhere,) * 2,
        scratch_shapes=scratch,
        input_output_aliases={} if fresh else {3: 0, 4: 1},
        compiler_params=pltpu.CompilerParams(vmem_limit_bytes=VMEM_BYTES),
        cost_estimate=pl.CostEstimate(
            flops=slots * tokens * BLK * BLK,
            bytes_accessed=slots * tokens * BLK * 2,
            transcendentals=0,
        ),
        name="tiles_here" if fresh else "tiles_moved",
    )(plan, rows, out_grad, *([] if fresh else partial))


def halving_order(owners):
    bits = [1 << i for i in range(owners.bit_length() - 1)]
    places = []
    for place in range(owners):
        relative = 0
        for i, bit in enumerate(bits):
            if place & (owners >> (i + 1)):
                relative |= bit
        places.append(relative)
    return bits, tuple(places)


def on_device(shards, owners, activations, out_grad, tile_list, tile_count):
    slots = tile_list.shape[1]
    row_blocks = activations.shape[1] // BLK
    col_blocks = out_grad.shape[1] // BLK
    here = lax.axis_index("mp")
    bits, order = halving_order(owners)

    row_ids = tile_list[0, :, 0]
    col_ids = tile_list[0, :, 1] - here * col_blocks
    live = jnp.arange(slots, dtype=jnp.int32) < tile_count[0]
    needed = jnp.where(live, row_ids, -1)
    lists = lax.all_gather(needed, "mp", axis=0, tiled=False)

    home = jnp.where(live, row_ids // row_blocks, -1)
    plan = jnp.stack([jnp.where(home == here, row_ids - here * row_blocks, -1), col_ids])
    partial = tiles(order, plan, activations, out_grad)

    all_blocks = jnp.arange(shards * row_blocks, dtype=jnp.int32)
    wanted = jnp.any(lists[:, :, None] == all_blocks, axis=1).astype(jnp.int32)
    wanted = wanted.reshape(shards, shards, row_blocks)
    counts = jnp.sum(wanted, axis=2)
    shard_ids = jnp.arange(shards, dtype=jnp.int32)
    mine = jnp.any(needed[:, None] == all_blocks, axis=0).astype(jnp.int32)
    mine = mine.reshape(shards, row_blocks)
    ranks = jnp.cumsum(mine, axis=1).reshape(-1) - 1
    rank = jnp.sum(jnp.where(needed[:, None] == all_blocks, ranks, 0), axis=1)

    for shift in range(1, shards):
        target = lax.rem(here + shift, shards)
        origin = lax.rem(here + shards - shift, shards)
        pairs = [(i, (i + shift) % shards) for i in range(shards)]
        on_way = shard_ids[:, None] == lax.rem(shard_ids + shift, shards)[None, :]
        most = jnp.max(jnp.where(on_way, counts, 0))
        outgoing = jnp.sum(
            jnp.where(
                (shard_ids[:, None, None] == target) & (shard_ids[None, :, None] == here), wanted, 0
            ),
            axis=(0, 1),
        )
        plan = jnp.stack([jnp.where(home == origin, rank, -1), col_ids])

        def move(count, outgoing, plan, partial, activations, out_grad):
            if count == 0:
                return partial
            packed = pack(outgoing, activations, count)
            arrived = lax.ppermute(packed, "mp", pairs)
            return tiles(order, plan, arrived, out_grad, partial)

        branches = [functools.partial(move, count) for count in range(min(row_blocks, slots) + 1)]
        partial = lax.switch(most, branches, outgoing, plan, partial, activations, out_grad)

    keep, send = partial
    for i, bit in enumerate(bits):
        arrived = lax.ppermute(send, "dp", [(d, d ^ bit) for d in range(owners)])
        if i + 1 < len(bits):
            middle = keep.shape[0] // 2
            keep, send = keep[:middle] + arrived[:middle], keep[middle:] + arrived[middle:]
        else:
            keep = keep + arrived
    return keep[None]


def solution(mesh):
    placed = (P("dp", "mp"), P("dp", "mp"), P("mp", None, None), P("mp"))
    return jax.shard_map(
        functools.partial(on_device, mesh.shape["mp"], mesh.shape["dp"]),
        mesh=mesh,
        in_specs=placed,
        out_specs=P("mp", "dp", None, None),
        check_vma=False,
    )
```

```python
import functools

import jax
import jax.numpy as jnp
from jax import lax
from jax.experimental import pallas as pl
from jax.experimental.pallas import tpu as pltpu
from jax.sharding import PartitionSpec as P

BLK = 128
VMEM_BYTES = 40 * 1024 * 1024
SCALARS = pl.BlockSpec(memory_space=pltpu.SMEM)
ANYWHERE = pl.BlockSpec(memory_space=pl.ANY)
IN_VMEM = pl.BlockSpec(memory_space=pltpu.VMEM)


def plan_kernel(shards, row_blocks, *refs):
    lists, (most_ref, send_ref, place_ref, seen) = refs[:shards], refs[shards:]
    slots = (lists[0].shape[0] - 1) // 2
    me = lax.axis_index("mp")

    def scan(list_ref, origin, note_slot, note_block):
        for b in range(row_blocks):
            seen[b] = -1

        def step(k, count):
            block = list_ref[2 * k] - origin * row_blocks
            wanted = (k < list_ref[2 * slots]) & (block >= 0) & (block < row_blocks)
            at = jnp.clip(block, 0, row_blocks - 1)
            new = wanted & (seen[at] < 0)

            @pl.when(new)
            def _():
                seen[at] = count
                note_block(count, at)

            note_slot(k, jnp.where(wanted, seen[at], -1))
            return count + new.astype(jnp.int32)

        return lax.fori_loop(0, slots, step, jnp.int32(0))

    def skip(*_):
        pass

    for shift in range(1, shards):
        for b in range(row_blocks):
            send_ref[(shift - 1) * row_blocks + b] = 0

        def note_block(count, block):
            send_ref[(shift - 1) * row_blocks + count] = block

        def note_slot(k, place):
            place_ref[(shift - 1) * slots + k] = place

        most = jnp.int32(0)
        for s in range(shards):
            origin = lax.rem(me - s - shift + 2 * shards, shards)
            count = scan(
                lists[s],
                origin,
                note_slot if s == 0 else skip,
                note_block if s == shards - shift else skip,
            )
            most = jnp.maximum(most, count)
        most_ref[shift - 1] = most


def make_plan(shards, row_blocks, lists):
    slots = (lists[0].shape[0] - 1) // 2
    return pl.pallas_call(
        functools.partial(plan_kernel, shards, row_blocks),
        out_shape=(
            jax.ShapeDtypeStruct((shards - 1,), jnp.int32),
            jax.ShapeDtypeStruct(((shards - 1) * row_blocks,), jnp.int32),
            jax.ShapeDtypeStruct(((shards - 1) * slots,), jnp.int32),
        ),
        in_specs=[SCALARS] * shards,
        out_specs=(SCALARS,) * 3,
        scratch_shapes=[pltpu.SMEM((row_blocks,), jnp.int32)],
        name="plan",
    )(*lists)


def pack_kernel(shift, row_blocks, send_ref, act_ref, out_ref, sems):
    def copy(j):
        block = send_ref[(shift - 1) * row_blocks + j]
        source = act_ref.at[:, pl.ds(pl.multiple_of(block * BLK, BLK), BLK)]
        return pltpu.make_async_copy(source, out_ref.at[j], sems.at[j])

    @pl.loop(0, out_ref.shape[0])
    def _(j):
        copy(j).start()

    @pl.loop(0, out_ref.shape[0])
    def _(j):
        copy(j).wait()


def pack(shift, row_blocks, send, activations, count):
    tokens = activations.shape[0]
    return pl.pallas_call(
        functools.partial(pack_kernel, shift, row_blocks),
        out_shape=jax.ShapeDtypeStruct((count, tokens, BLK), activations.dtype),
        in_specs=[SCALARS, ANYWHERE],
        out_specs=IN_VMEM,
        scratch_shapes=[pltpu.SemaphoreType.DMA((count,))],
        cost_estimate=pl.CostEstimate(
            flops=0, bytes_accessed=count * tokens * BLK * 4, transcendentals=0
        ),
        name="pack",
    )(send, activations)


def tiles_kernel(owners, row_blocks, shift, list_ref, place_ref, rows_ref, grad_ref, *rest):
    if shift:
        rest = rest[2:]
    keep_ref, send_ref, row_buf, grad_buf, stage, row_sems, grad_sems, out_sems = rest
    slots = (list_ref.shape[0] - 1) // 2
    half = slots // 2
    lanes = slots // owners
    steps = owners.bit_length() - 1
    depth = row_buf.shape[0]
    me = lax.axis_index("dp")
    shard = lax.axis_index("mp")
    col_blocks = grad_ref.shape[1] // BLK

    def slot_of(place):
        owner = place // lanes
        relative = jnp.int32(0)
        for i in range(steps):
            relative = relative | (((owner >> (steps - 1 - i)) & 1) << i)
        return (me ^ relative) * lanes + place % lanes

    def block_of(slot):
        if shift:
            return place_ref[(shift - 1) * slots + slot]
        block = list_ref[2 * slot] - shard * row_blocks
        here = (block >= 0) & (block < row_blocks) & (slot < list_ref[2 * slots])
        return jnp.where(here, block, -1)

    def loads(place):
        slot = slot_of(place)
        block = block_of(slot)
        at = lax.rem(place, depth)
        first = jnp.maximum(block, 0)
        if shift:
            source = rows_ref.at[first]
        else:
            source = rows_ref.at[:, pl.ds(pl.multiple_of(first * BLK, BLK), BLK)]
        column = list_ref[2 * slot + 1] - shard * col_blocks
        return (
            block >= 0,
            pltpu.make_async_copy(source, row_buf.at[at], row_sems.at[at]),
            pltpu.make_async_copy(
                grad_ref.at[:, pl.ds(pl.multiple_of(column * BLK, BLK), BLK)],
                grad_buf.at[at],
                grad_sems.at[at],
            ),
        )

    def start(place):
        used, row_copy, grad_copy = loads(place)

        @pl.when(used)
        def _():
            row_copy.start()
            grad_copy.start()

    def out_copy(place, act):
        @pl.when(place < half)
        def _():
            act(pltpu.make_async_copy(stage.at[place], keep_ref.at[place], out_sems.at[place]))

        @pl.when(place >= half)
        def _():
            act(
                pltpu.make_async_copy(stage.at[place], send_ref.at[place - half], out_sems.at[place])
            )

    @pl.loop(0, depth)
    def _(place):
        start(place)

    @pl.loop(0, slots)
    def _(place):
        used, row_copy, grad_copy = loads(place)
        at = lax.rem(place, depth)

        @pl.when(used)
        def _():
            row_copy.wait()
            grad_copy.wait()
            stage[place] = lax.dot_general(
                row_buf[at],
                grad_buf[at],
                (((0,), (0,)), ((), ())),
                preferred_element_type=jnp.float32,
            )

        if not shift:

            @pl.when(jnp.logical_not(used))
            def _():
                stage[place] = jnp.zeros((BLK, BLK), jnp.float32)

            out_copy(place, lambda copy: copy.start())
        else:

            @pl.when(used)
            def _():
                out_copy(place, lambda copy: copy.start())

        if depth < slots:
            pl.when(place + depth < slots)(lambda: start(place + depth))

    @pl.loop(0, slots)
    def _(place):
        if shift:

            @pl.when(block_of(slot_of(place)) >= 0)
            def _():
                out_copy(place, lambda copy: copy.wait())
        else:
            out_copy(place, lambda copy: copy.wait())


def tiles(owners, row_blocks, shift, slot_list, places, rows, out_grad, partial=()):
    tokens = out_grad.shape[0]
    slots = (slot_list.shape[0] - 1) // 2
    depth = min(slots, 16)
    half = jax.ShapeDtypeStruct((slots // 2, BLK, BLK), jnp.float32)
    return pl.pallas_call(
        functools.partial(tiles_kernel, owners, row_blocks, shift),
        out_shape=(half, half),
        in_specs=[SCALARS, SCALARS, ANYWHERE, ANYWHERE] + [ANYWHERE] * len(partial),
        out_specs=(ANYWHERE,) * 2,
        scratch_shapes=[
            pltpu.VMEM((depth, tokens, BLK), rows.dtype),
            pltpu.VMEM((depth, tokens, BLK), out_grad.dtype),
            pltpu.VMEM((slots, BLK, BLK), jnp.float32),
            pltpu.SemaphoreType.DMA((depth,)),
            pltpu.SemaphoreType.DMA((depth,)),
            pltpu.SemaphoreType.DMA((slots,)),
        ],
        input_output_aliases={4: 0, 5: 1} if partial else {},
        compiler_params=pltpu.CompilerParams(vmem_limit_bytes=VMEM_BYTES),
        cost_estimate=pl.CostEstimate(
            flops=slots * tokens * BLK * BLK,
            bytes_accessed=slots * tokens * BLK * 2,
            transcendentals=0,
        ),
        name="tiles_moved" if shift else "tiles_here",
    )(slot_list, places, rows, out_grad, *partial)


def on_device(shards, owners, activations, out_grad, tile_list, tile_count):
    slots = tile_list.shape[1]
    row_blocks = activations.shape[1] // BLK

    slot_list = jnp.concatenate([tile_list.reshape(-1), tile_count])
    routes = [[(i, (i + s) % shards) for i in range(shards)] for s in range(shards)]
    lists = [slot_list] + [lax.ppermute(slot_list, "mp", routes[s]) for s in range(1, shards)]
    partial = tiles(owners, row_blocks, 0, slot_list, slot_list, activations, out_grad)
    most, send, places = make_plan(shards, row_blocks, lists)

    for shift in range(1, shards):

        def move(count, send, slot_list, places, partial, activations, out_grad):
            if count == 0:
                return partial
            packed = pack(shift, row_blocks, send, activations, count)
            arrived = lax.ppermute(packed, "mp", routes[shift])
            return tiles(owners, row_blocks, shift, slot_list, places, arrived, out_grad, partial)

        branches = [functools.partial(move, count) for count in range(min(row_blocks, slots) + 1)]
        partial = lax.switch(
            most[shift - 1], branches, send, slot_list, places, partial, activations, out_grad
        )

    keep, send = partial
    steps = owners.bit_length() - 1
    for i in range(steps):
        arrived = lax.ppermute(send, "dp", [(d, d ^ (1 << i)) for d in range(owners)])
        if i + 1 < steps:
            middle = keep.shape[0] // 2
            keep, send = keep[:middle] + arrived[:middle], keep[middle:] + arrived[middle:]
        else:
            keep = keep + arrived
    return keep[None]


def solution(mesh):
    placed = (P("dp", "mp"), P("dp", "mp"), P("mp", None, None), P("mp"))
    return jax.shard_map(
        functools.partial(on_device, mesh.shape["mp"], mesh.shape["dp"]),
        mesh=mesh,
        in_specs=placed,
        out_specs=P("mp", "dp", None, None),
        check_vma=False,
    )
```

```python
import functools

import jax
import jax.numpy as jnp
from jax import lax
from jax.experimental import pallas as pl
from jax.experimental.pallas import tpu as pltpu
from jax.sharding import PartitionSpec as P

BLK = 128
MIB = 1024 * 1024
SCALARS = pl.BlockSpec(memory_space=pltpu.SMEM)
ANYWHERE = pl.BlockSpec(memory_space=pl.ANY)
IN_VMEM = pl.BlockSpec(memory_space=pltpu.VMEM)


def first_seen(slots, row_blocks, origin, list_ref, seen, note_slot, note_block):
    for b in range(row_blocks):
        seen[b] = -1

    def step(k, count):
        block = list_ref[k] - origin * row_blocks

        @pl.when((block >= 0) & (block < row_blocks))
        def _():
            known = seen[block]
            place = jnp.where(known < 0, count, known)
            seen[block] = place
            note_slot(k, place)
            note_block(place, block)

        at = jnp.clip(block, 0, row_blocks - 1)
        return jnp.where((block >= 0) & (block < row_blocks), jnp.maximum(count, seen[at] + 1), count)

    return lax.fori_loop(0, list_ref[2 * slots], step, jnp.int32(0))


def skip(*_):
    pass


def need_kernel(shards, row_blocks, list_ref, need_ref, seen):
    slots = (list_ref.shape[0] - 1) // 2
    shard = lax.axis_index("mp")
    for shift in range(1, shards):
        origin = lax.rem(shard + shards - shift, shards)
        need_ref[shift - 1] = first_seen(slots, row_blocks, origin, list_ref, seen, skip, skip)


def count_needed(shards, row_blocks, slot_list):
    return pl.pallas_call(
        functools.partial(need_kernel, shards, row_blocks),
        out_shape=jax.ShapeDtypeStruct((shards - 1,), jnp.int32),
        in_specs=[SCALARS],
        out_specs=SCALARS,
        scratch_shapes=[pltpu.SMEM((row_blocks,), jnp.int32)],
        name="need",
    )(slot_list)


def jobs_kernel(shards, owners, row_blocks, col_blocks, list_ref, job_ref, size_ref, seen):
    slots = (list_ref.shape[0] - 1) // 2
    lanes = slots // owners
    steps = owners.bit_length() - 1
    me = lax.axis_index("dp")
    shard = lax.axis_index("mp")
    for shift in range(shards):
        base = shift * slots * 3
        size_ref[shift] = 0

        def note_slot(k, block):
            relative = (k // lanes) ^ me
            place = jnp.int32(0)
            for i in range(steps):
                place = place | (((relative >> i) & 1) << (steps - 1 - i))
            job = size_ref[shift]
            job_ref[base + 3 * job] = place * lanes + k % lanes
            job_ref[base + 3 * job + 1] = block
            job_ref[base + 3 * job + 2] = list_ref[slots + k] - shard * col_blocks
            size_ref[shift] = job + 1

        if shift:
            origin = lax.rem(shard + shards - shift, shards)
            first_seen(slots, row_blocks, origin, list_ref, seen, note_slot, skip)
        else:

            @pl.loop(0, list_ref[2 * slots])
            def _(k):
                block = list_ref[k] - shard * row_blocks

                @pl.when((block >= 0) & (block < row_blocks))
                def _():
                    note_slot(k, block)


def make_jobs(shards, owners, row_blocks, col_blocks, slot_list):
    slots = (slot_list.shape[0] - 1) // 2
    return pl.pallas_call(
        functools.partial(jobs_kernel, shards, owners, row_blocks, col_blocks),
        out_shape=(
            jax.ShapeDtypeStruct((shards * slots * 3,), jnp.int32),
            jax.ShapeDtypeStruct((shards,), jnp.int32),
        ),
        in_specs=[SCALARS],
        out_specs=(SCALARS,) * 2,
        scratch_shapes=[pltpu.SMEM((row_blocks,), jnp.int32)],
        name="jobs",
    )(slot_list)


def plan_kernel(shards, row_blocks, need_ref, *refs):
    lists, (most_ref, send_ref, seen) = refs[: shards - 1], refs[shards - 1 :]
    slots = (lists[0].shape[0] - 1) // 2
    me = lax.axis_index("mp")
    for shift in range(1, shards):
        for b in range(row_blocks):
            send_ref[(shift - 1) * row_blocks + b] = 0

        def note_block(place, block):
            send_ref[(shift - 1) * row_blocks + place] = block

        most = need_ref[shift - 1]
        for s in range(1, shards):
            origin = lax.rem(me - s - shift + 2 * shards, shards)
            note = note_block if s == shards - shift else skip
            count = first_seen(slots, row_blocks, origin, lists[s - 1], seen, skip, note)
            most = jnp.maximum(most, count)
        most_ref[shift - 1] = most


def make_plan(shards, row_blocks, need, lists):
    return pl.pallas_call(
        functools.partial(plan_kernel, shards, row_blocks),
        out_shape=(
            jax.ShapeDtypeStruct((shards - 1,), jnp.int32),
            jax.ShapeDtypeStruct(((shards - 1) * row_blocks,), jnp.int32),
        ),
        in_specs=[SCALARS] * shards,
        out_specs=(SCALARS,) * 2,
        scratch_shapes=[pltpu.SMEM((row_blocks,), jnp.int32)],
        name="plan",
    )(need, *lists)


def pack_kernel(shift, row_blocks, send_ref, act_ref, *rest):
    *out_refs, sems = rest

    def each(act):
        first = 0
        for out_ref in out_refs:

            @pl.loop(0, out_ref.shape[0])
            def _(j):
                source = column(act_ref, send_ref[(shift - 1) * row_blocks + first + j])
                act(pltpu.make_async_copy(source, out_ref.at[j], sems.at[first + j]))

            first += out_ref.shape[0]

    each(begin)
    each(finish)


def pack(shift, row_blocks, sizes, send, activations):
    tokens = activations.shape[0]
    count = sum(sizes)
    return pl.pallas_call(
        functools.partial(pack_kernel, shift, row_blocks),
        out_shape=tuple(pltpu.VMEM((size, tokens, BLK), activations.dtype) for size in sizes),
        in_specs=[SCALARS, ANYWHERE],
        out_specs=(IN_VMEM,) * len(sizes),
        scratch_shapes=[pltpu.SemaphoreType.DMA((count,))],
        compiler_params=pltpu.CompilerParams(vmem_limit_bytes=4 * MIB),
        cost_estimate=pl.CostEstimate(
            flops=0, bytes_accessed=count * tokens * BLK * 4, transcendentals=0
        ),
        name="pack",
    )(send, activations)


def multiply(rows, cols):
    return lax.dot_general(
        rows, cols, (((0,), (0,)), ((), ())), preferred_element_type=jnp.float32
    )


def column(ref, block):
    return ref.at[:, pl.ds(pl.multiple_of(block * BLK, BLK), BLK)]


def out_copy(stage, keep_ref, send_ref, sems, place, act):
    half = keep_ref.shape[0]

    @pl.when(place < half)
    def _():
        act(pltpu.make_async_copy(stage.at[place], keep_ref.at[place], sems.at[place]))

    @pl.when(place >= half)
    def _():
        act(pltpu.make_async_copy(stage.at[place], send_ref.at[place - half], sems.at[place]))


def begin(copy):
    copy.start()


def finish(copy):
    copy.wait()


def here_kernel(shards, job_ref, size_ref, act_ref, grad_ref, *rest):
    _, _, keep_ref, send_ref, later_ref, row_buf, col_buf, stage, *sems = rest
    row_sems, col_sems, later_sems, out_sems = sems
    slots = later_ref.shape[0]
    depth = col_buf.shape[0]
    jobs = size_ref[0]
    out = functools.partial(out_copy, stage, keep_ref, send_ref, out_sems)

    def row_copy(job):
        at = lax.rem(job, depth)
        source = column(act_ref, job_ref[3 * job + 1])
        return pltpu.make_async_copy(source, row_buf.at[at], row_sems.at[at])

    def col_copy(job):
        at = lax.rem(job, depth)
        source = column(grad_ref, job_ref[3 * job + 2])
        return pltpu.make_async_copy(source, col_buf.at[at], col_sems.at[at])

    def each_later(act):
        before = jnp.int32(0)
        for shift in range(1, shards):

            @pl.loop(0, size_ref[shift])
            def _(job):
                source = column(grad_ref, job_ref[3 * (shift * slots + job) + 2])
                at = before + job
                act(pltpu.make_async_copy(source, later_ref.at[at], later_sems.at[at]))

            before = before + size_ref[shift]

    def start(job):
        row_copy(job).start()
        col_copy(job).start()

    pl.loop(0, jnp.minimum(depth, jobs))(start)
    each_later(begin)

    @pl.loop(0, jobs)
    def _(job):
        at = lax.rem(job, depth)
        place = job_ref[3 * job]
        row_copy(job).wait()
        col_copy(job).wait()
        stage[place] = multiply(row_buf[at], col_buf[at])
        out(place, begin)
        if depth < slots:
            pl.when(job + depth < jobs)(lambda: start(job + depth))

    each_later(finish)

    @pl.loop(0, jobs)
    def _(job):
        out(job_ref[3 * job], finish)


def products_here(shards, slots, jobs, sizes, activations, out_grad, partial):
    tokens = out_grad.shape[0]
    depth = min(slots, 16)
    half = jax.ShapeDtypeStruct((slots // 2, BLK, BLK), jnp.float32)
    room = 2 * depth * tokens * BLK * 2 + slots * BLK * BLK * 4 + 4 * MIB
    return pl.pallas_call(
        functools.partial(here_kernel, shards),
        out_shape=(half, half, jax.ShapeDtypeStruct((slots, tokens, BLK), out_grad.dtype)),
        in_specs=[SCALARS] * 2 + [ANYWHERE] * 4,
        out_specs=(ANYWHERE,) * 3,
        scratch_shapes=[
            pltpu.VMEM((depth, tokens, BLK), activations.dtype),
            pltpu.VMEM((depth, tokens, BLK), out_grad.dtype),
            pltpu.VMEM((slots, BLK, BLK), jnp.float32),
            pltpu.SemaphoreType.DMA((depth,)),
            pltpu.SemaphoreType.DMA((depth,)),
            pltpu.SemaphoreType.DMA((slots,)),
            pltpu.SemaphoreType.DMA((slots,)),
        ],
        input_output_aliases={4: 0, 5: 1},
        compiler_params=pltpu.CompilerParams(vmem_limit_bytes=room),
        cost_estimate=pl.CostEstimate(
            flops=slots * tokens * BLK * BLK,
            bytes_accessed=slots * tokens * BLK * 4,
            transcendentals=0,
        ),
        name="products_here",
    )(jobs, sizes, activations, out_grad, *partial)


def moved_kernel(shift, first, job_ref, size_ref, rows_ref, cols_ref, *rest):
    _, _, keep_ref, send_ref, stage, out_sems = rest
    slots = cols_ref.shape[0]
    out = functools.partial(out_copy, stage, keep_ref, send_ref, out_sems)
    before = jnp.int32(0)
    for earlier in range(1, shift):
        before = before + size_ref[earlier]

    def each_job(act):
        @pl.loop(0, size_ref[shift])
        def _(job):
            base = 3 * (shift * slots + job)
            block = job_ref[base + 1] - first

            @pl.when((block >= 0) & (block < rows_ref.shape[0]))
            def _():
                act(job, job_ref[base], block)

    def work(job, place, block):
        stage[place] = multiply(rows_ref[block], cols_ref[before + job])
        out(place, begin)

    each_job(work)
    each_job(lambda _, place, __: out(place, finish))


def products_moved(shift, first, jobs, sizes, rows, cols, partial):
    slots, tokens = cols.shape[:2]
    half = jax.ShapeDtypeStruct((slots // 2, BLK, BLK), jnp.float32)
    room = (rows.shape[0] + slots) * tokens * BLK * 2 + slots * BLK * BLK * 4 + 4 * MIB
    return pl.pallas_call(
        functools.partial(moved_kernel, shift, first),
        out_shape=(half, half),
        in_specs=[SCALARS] * 2 + [IN_VMEM] * 2 + [ANYWHERE] * 2,
        out_specs=(ANYWHERE,) * 2,
        scratch_shapes=[
            pltpu.VMEM((slots, BLK, BLK), jnp.float32),
            pltpu.SemaphoreType.DMA((slots,)),
        ],
        input_output_aliases={4: 0, 5: 1},
        compiler_params=pltpu.CompilerParams(vmem_limit_bytes=room),
        cost_estimate=pl.CostEstimate(
            flops=slots * tokens * BLK * BLK,
            bytes_accessed=slots * tokens * BLK * 4,
            transcendentals=0,
        ),
        name="products_moved",
    )(jobs, sizes, rows, cols, *partial)


def reduce_to_owner(owners, keep, send):
    lanes = (keep.shape[0] + send.shape[0]) // owners
    steps = owners.bit_length() - 1

    def swap(part, mask):
        return lax.ppermute(part, "dp", [(d, d ^ mask) for d in range(owners)])

    def halve(part, i):
        middle = part[0].shape[0] // 2
        arrived = swap(part[1], 1 << i)
        return [part[0][:middle] + arrived[:middle], part[0][middle:] + arrived[middle:]]

    if steps < 4:
        part = [keep, send]
        for i in range(steps - 1):
            part = halve(part, i)
        return part[0] + swap(part[1], 1 << (steps - 1))

    part = [keep, send]
    for i in range(steps - 4):
        part = halve(part, i)
    keep = part[0]
    came = swap(part[1], 1 << (steps - 4))

    def chunk(first):
        held = slice(first * lanes, (first + 2) * lanes)
        sent = slice((first + 4) * lanes, (first + 6) * lanes)
        return keep[held] + came[held], swap(keep[sent] + came[sent], 1 << (steps - 3))

    far_keep, far_came = chunk(2)
    near_keep, near_came = chunk(0)
    low, high = 1 << (steps - 2), 1 << (steps - 1)
    both_came = swap(far_keep[lanes:] + far_came[lanes:], low | high)
    low_came = swap(far_keep[:lanes] + far_came[:lanes], low)
    high_came = swap(near_keep[lanes:] + near_came[lanes:], high)
    return near_keep[:lanes] + near_came[:lanes] + both_came + low_came + high_came


def on_device(shards, owners, activations, out_grad, tile_list, tile_count):
    slots = tile_list.shape[1]
    row_blocks = activations.shape[1] // BLK
    col_blocks = out_grad.shape[1] // BLK

    slot_list = jnp.concatenate([tile_list[0, :, 0], tile_list[0, :, 1], tile_count])
    routes = [[(i, (i + s) % shards) for i in range(shards)] for s in range(shards)]
    lists = [lax.ppermute(slot_list, "mp", routes[s]) for s in range(1, shards)]
    need = count_needed(shards, row_blocks, slot_list)
    most, send = make_plan(shards, row_blocks, need, lists)

    carried = ()
    for shift in range(1, shards):

        def move(count, send, slot_list, carried, activations, out_grad):
            sizes = [count] if count < 2 else [count - 1, 1]
            packed = pack(shift, row_blocks, sizes, send, activations) if count else ()
            arrived = [lax.ppermute(part, "mp", routes[shift]) for part in packed]
            jobs, amounts = make_jobs(shards, owners, row_blocks, col_blocks, slot_list)
            if shift == 1:
                blank = jnp.zeros((slots // 2, BLK, BLK), jnp.float32)
                blank = lax.optimization_barrier((blank, blank))
                *partial, later = products_here(
                    shards, slots, jobs, amounts, activations, out_grad, blank
                )
            else:
                *partial, later = carried
            for n, rows in enumerate(arrived):
                partial = products_moved(
                    shift, sum(sizes[:n]), jobs, amounts, rows, later, partial
                )
            if shift + 1 < shards:
                return *partial, later
            return reduce_to_owner(owners, *partial)[None]

        carried = lax.switch(
            most[shift - 1],
            [functools.partial(move, count) for count in range(min(row_blocks, slots) + 1)],
            send,
            slot_list,
            carried,
            activations,
            out_grad,
        )
    return carried


def solution(mesh):
    placed = (P("dp", "mp"), P("dp", "mp"), P("mp", None, None), P("mp"))
    return jax.shard_map(
        functools.partial(on_device, mesh.shape["mp"], mesh.shape["dp"]),
        mesh=mesh,
        in_specs=placed,
        out_specs=P("mp", "dp", None, None),
        check_vma=False,
    )
```

```python
import functools

import jax
import jax.numpy as jnp
from jax import lax
from jax.experimental import pallas as pl
from jax.experimental.pallas import tpu as pltpu
from jax.sharding import PartitionSpec as P

BLK = 128
MIB = 1024 * 1024
SCALARS = pl.BlockSpec(memory_space=pltpu.SMEM)
ANYWHERE = pl.BlockSpec(memory_space=pl.ANY)
IN_VMEM = pl.BlockSpec(memory_space=pltpu.VMEM)


def skip(*_):
    pass


def scan(slots, row_blocks, origin, list_ref, note=skip, without=(), first=0):
    def step(k, state):
        count, once, twice = state
        block = list_ref[k] - origin * row_blocks
        wanted = (k < list_ref[2 * slots]) & (block >= 0) & (block < row_blocks)
        for other in without:
            wanted = wanted & (k != other)
        bit = jnp.where(wanted, jnp.int32(1) << (block & 31), 0)
        new = ((once & bit) == 0) & wanted
        note(jnp.where(new, count, row_blocks), block)
        return count + new.astype(jnp.int32), once | bit, twice | (once & bit)

    state = jnp.int32(first), jnp.int32(0), jnp.int32(0)
    return lax.fori_loop(0, slots, step, state, unroll=slots <= 16)


def plan_kernel(shards, row_blocks, sizes, *refs):
    lists, (branch_ref, send_ref, host_ref) = refs[:shards], refs[shards:]
    slots = (lists[0].shape[0] - 1) // 2
    me = lax.axis_index("mp")
    for n in range(5):
        host_ref[n] = -1 if n < 4 else 0
    for shift in range(1, shards):
        for b in range(row_blocks):
            send_ref[(shift - 1) * (row_blocks + 1) + b] = 0

        def note_block(place, block):
            send_ref[(shift - 1) * (row_blocks + 1) + place] = block

        most = jnp.int32(0)
        for s in range(shards):
            origin = lax.rem(me - s - shift + 2 * shards, shards)
            note = note_block if s == shards - shift else skip
            most = jnp.maximum(most, scan(slots, row_blocks, origin, lists[s], note)[0])
        branch_ref[shift - 1] = sum((most > size).astype(jnp.int32) for size in sizes[:-1])


def pair_plan_kernel(row_blocks, col_blocks, sizes, hosted_sizes, *refs):
    mine_ref, theirs_ref, branch_ref, send_ref, host_ref = refs
    slots = (mine_ref.shape[0] - 1) // 2
    me = lax.axis_index("mp")
    my_need, my_once, my_twice = scan(slots, row_blocks, 1 - me, mine_ref)
    their_need, their_once, their_twice = scan(slots, row_blocks, me, theirs_ref)
    i_am_heavy = my_need > their_need
    heavy, light = jnp.maximum(my_need, their_need), jnp.minimum(my_need, their_need)
    single = jnp.where(i_am_heavy, my_once & ~my_twice, their_once & ~their_twice)
    singles = sum((single >> b) & 1 for b in range(row_blocks))

    best, hosted, height = 4 * heavy, jnp.int32(0), heavy
    for count in (1, 2):
        level = jnp.maximum(jnp.maximum(heavy - count, light + count), hosted_sizes[0])
        cost = 4 * level + 2
        better = (singles >= count) & (level <= hosted_sizes[-1]) & (cost < best)
        best = jnp.where(better, cost, best)
        hosted = jnp.where(better, count, hosted)
        height = jnp.where(better, level, height)
    plain = sum((height > size).astype(jnp.int32) for size in sizes[:-1])
    shared = sum((height > size).astype(jnp.int32) for size in hosted_sizes[:-1])
    branch_ref[0] = jnp.where(hosted > 0, len(sizes) + shared, plain)

    def picks(list_ref, origin, count):
        def step(k, state):
            found, one, two = state
            block = list_ref[k] - origin * row_blocks
            fits = (k < list_ref[2 * slots]) & (block >= 0) & (block < row_blocks)
            fits = fits & (((single >> (block & 31)) & 1) > 0) & (found < count)
            one = jnp.where(fits & (found == 0), k, one)
            two = jnp.where(fits & (found == 1), k, two)
            return found + fits.astype(jnp.int32), one, two

        state = jnp.int32(0), jnp.int32(-1), jnp.int32(-1)
        return lax.fori_loop(0, slots, step, state, unroll=slots <= 16)[1:]

    my_picks = picks(mine_ref, 1 - me, jnp.where(i_am_heavy, hosted, 0))
    their_picks = picks(theirs_ref, me, jnp.where(i_am_heavy, 0, hosted))
    for b in range(row_blocks):
        send_ref[b] = 0
    for n in range(2):
        host_ref[n] = my_picks[n]
        row = theirs_ref[jnp.maximum(their_picks[n], 0)] - me * row_blocks
        host_ref[2 + n] = jnp.where(their_picks[n] >= 0, row, -1)
        col = mine_ref[slots + jnp.maximum(my_picks[n], 0)] - me * col_blocks
        send_ref[jnp.where(my_picks[n] >= 0, n, row_blocks)] = row_blocks + col
    host_ref[4] = jnp.where(i_am_heavy, 0, hosted)

    def note_block(place, block):
        send_ref[place] = block

    ahead = jnp.where(i_am_heavy, hosted, 0)
    scan(slots, row_blocks, me, theirs_ref, note_block, their_picks, ahead)


def make_plan(shards, row_blocks, col_blocks, sizes, hosted_sizes, lists):
    kernel = functools.partial(plan_kernel, shards, row_blocks, sizes)
    if hosted_sizes:
        kernel = functools.partial(pair_plan_kernel, row_blocks, col_blocks, sizes, hosted_sizes)
    return pl.pallas_call(
        kernel,
        out_shape=(
            jax.ShapeDtypeStruct((shards - 1,), jnp.int32),
            jax.ShapeDtypeStruct(((shards - 1) * (row_blocks + 1),), jnp.int32),
            jax.ShapeDtypeStruct((5,), jnp.int32),
        ),
        in_specs=[SCALARS] * shards,
        out_specs=(SCALARS,) * 3,
        name="plan",
    )(*lists)


def jobs_kernel(shards, owners, row_blocks, col_blocks, list_ref, host_ref, job_ref, size_ref, seen):
    slots = (list_ref.shape[0] - 1) // 2
    lanes = slots // owners
    steps = owners.bit_length() - 1
    me = lax.axis_index("dp")
    shard = lax.axis_index("mp")

    def place_of(k):
        relative = (k // lanes) ^ me
        place = jnp.int32(0)
        for i in range(steps):
            place = place | (((relative >> i) & 1) << (steps - 1 - i))
        return place * lanes + k % lanes

    for n in range(2):
        slot = host_ref[n]
        size_ref[shards + n] = jnp.where(slot >= 0, place_of(jnp.maximum(slot, 0)), -1)
    for shift in range(shards):
        base = shift * slots * 3
        size_ref[shift] = 0
        origin = lax.rem(shard + shards - shift, shards)
        first = host_ref[4] if shift else 0
        if shift:
            for b in range(row_blocks):
                seen[b] = -1

        def step(k, count):
            block = list_ref[k] - origin * row_blocks
            wanted = (block >= 0) & (block < row_blocks)
            wanted = wanted & (k != host_ref[0]) & (k != host_ref[1])

            @pl.when(wanted)
            def _():
                source = block
                if shift:
                    known = seen[block]
                    source = jnp.where(known < 0, count, known)
                    seen[block] = source
                job = size_ref[shift]
                job_ref[base + 3 * job] = place_of(k)
                job_ref[base + 3 * job + 1] = source
                job_ref[base + 3 * job + 2] = list_ref[slots + k] - shard * col_blocks
                size_ref[shift] = job + 1

            at = jnp.clip(block, 0, row_blocks - 1)
            return jnp.where(wanted, jnp.maximum(count, seen[at] + 1), count)

        lax.fori_loop(0, list_ref[2 * slots], step, first)


def make_jobs(shards, owners, row_blocks, col_blocks, slot_list, host):
    slots = (slot_list.shape[0] - 1) // 2
    return pl.pallas_call(
        functools.partial(jobs_kernel, shards, owners, row_blocks, col_blocks),
        out_shape=(
            jax.ShapeDtypeStruct((shards * slots * 3,), jnp.int32),
            jax.ShapeDtypeStruct((shards + 2,), jnp.int32),
        ),
        in_specs=[SCALARS] * 2,
        out_specs=(SCALARS,) * 2,
        scratch_shapes=[pltpu.SMEM((row_blocks,), jnp.int32)],
        cost_estimate=pl.CostEstimate(flops=0, bytes_accessed=1 << 20, transcendentals=0),
        name="jobs",
    )(slot_list, host)


def pack_kernel(shift, row_blocks, mixed, send_ref, act_ref, *rest):
    *out_refs, buf, in_sems, out_sems = rest[1:] if mixed else rest
    count = buf.shape[0]

    @pl.loop(0, count)
    def _(j):
        block = send_ref[(shift - 1) * (row_blocks + 1) + j]

        def fetch(source):
            pltpu.make_async_copy(source, buf.at[j], in_sems.at[j]).start()

        if mixed:
            pl.when(block < row_blocks)(lambda: fetch(column(act_ref, block)))
            pl.when(block >= row_blocks)(lambda: fetch(column(rest[0], block - row_blocks)))
        else:
            fetch(column(act_ref, block))

    def each_out(act):
        first = 0
        for out_ref in out_refs:

            @pl.loop(0, out_ref.shape[0])
            def _(j):
                at = first + j
                act(at, pltpu.make_async_copy(buf.at[at], out_ref.at[j], out_sems.at[at]))

            first += out_ref.shape[0]

    def pass_on(at, copy):
        pltpu.make_async_copy(column(act_ref, 0), buf.at[at], in_sems.at[at]).wait()
        copy.start()

    each_out(pass_on)
    each_out(lambda _, copy: copy.wait())


def pack(shift, row_blocks, sizes, send, activations, *out_grad):
    tokens = activations.shape[0]
    count = sum(sizes)
    return pl.pallas_call(
        functools.partial(pack_kernel, shift, row_blocks, bool(out_grad)),
        out_shape=tuple(
            jax.ShapeDtypeStruct((size, tokens, BLK), activations.dtype) for size in sizes
        ),
        in_specs=[SCALARS] + [ANYWHERE] * (1 + len(out_grad)),
        out_specs=(ANYWHERE,) * len(sizes),
        scratch_shapes=[
            pltpu.VMEM((count, tokens, BLK), activations.dtype),
            pltpu.SemaphoreType.DMA((count,)),
            pltpu.SemaphoreType.DMA((count,)),
        ],
        compiler_params=pltpu.CompilerParams(
            vmem_limit_bytes=count * tokens * BLK * 2 + 2 * MIB
        ),
        cost_estimate=pl.CostEstimate(
            flops=0, bytes_accessed=count * tokens * BLK * 4, transcendentals=0
        ),
        name="pack",
    )(send, activations, *out_grad)


def multiply(rows, cols):
    return lax.dot_general(
        rows, cols, (((0,), (0,)), ((), ())), preferred_element_type=jnp.float32
    )


def column(ref, block):
    return ref.at[:, pl.ds(pl.multiple_of(block * BLK, BLK), BLK)]


def out_copy(stage, keep_ref, send_ref, sems, place, act, at=None):
    half = keep_ref.shape[0]
    at = place if at is None else at

    @pl.when(place < half)
    def _():
        act(pltpu.make_async_copy(stage.at[at], keep_ref.at[place], sems.at[place]))

    @pl.when(place >= half)
    def _():
        act(pltpu.make_async_copy(stage.at[at], send_ref.at[place - half], sems.at[place]))


def begin(copy):
    copy.start()


def finish(copy):
    copy.wait()


def here_kernel(shards, job_ref, size_ref, act_ref, grad_ref, *rest):
    _, _, keep_ref, send_ref, later_ref, row_buf, col_buf, stage, *sems = rest
    row_sems, col_sems, later_sems, out_sems = sems
    slots = later_ref.shape[0]
    depth = col_buf.shape[0]
    jobs = size_ref[0]
    out = functools.partial(out_copy, stage, keep_ref, send_ref, out_sems)

    def row_copy(job):
        at = lax.rem(job, depth)
        source = column(act_ref, job_ref[3 * job + 1])
        return pltpu.make_async_copy(source, row_buf.at[at], row_sems.at[at])

    def col_copy(job):
        at = lax.rem(job, depth)
        source = column(grad_ref, job_ref[3 * job + 2])
        return pltpu.make_async_copy(source, col_buf.at[at], col_sems.at[at])

    def each_later(act):
        before = jnp.int32(0)
        for shift in range(1, shards):

            @pl.loop(0, size_ref[shift])
            def _(job):
                source = column(grad_ref, job_ref[3 * (shift * slots + job) + 2])
                at = before + job
                act(pltpu.make_async_copy(source, later_ref.at[at], later_sems.at[at]))

            before = before + size_ref[shift]

    def start(job):
        row_copy(job).start()
        col_copy(job).start()

    pl.loop(0, jnp.minimum(depth, jobs))(start)
    each_later(begin)

    @pl.loop(0, jobs)
    def _(job):
        at = lax.rem(job, depth)
        place = job_ref[3 * job]
        row_copy(job).wait()
        col_copy(job).wait()
        stage[place] = multiply(row_buf[at], col_buf[at])
        out(place, begin)
        if depth < slots:
            pl.when(job + depth < jobs)(lambda: start(job + depth))

    each_later(finish)

    @pl.loop(0, jobs)
    def _(job):
        out(job_ref[3 * job], finish)


def products_here(shards, slots, jobs, sizes, activations, out_grad, partial):
    tokens = out_grad.shape[0]
    depth = min(slots, 8)
    half = jax.ShapeDtypeStruct((slots // 2, BLK, BLK), jnp.float32)
    room = 2 * depth * tokens * BLK * 2 + slots * BLK * BLK * 4 + 4 * MIB
    return pl.pallas_call(
        functools.partial(here_kernel, shards),
        out_shape=(half, half, jax.ShapeDtypeStruct((slots, tokens, BLK), out_grad.dtype)),
        in_specs=[SCALARS] * 2 + [ANYWHERE] * 4,
        out_specs=(ANYWHERE,) * 3,
        scratch_shapes=[
            pltpu.VMEM((depth, tokens, BLK), activations.dtype),
            pltpu.VMEM((depth, tokens, BLK), out_grad.dtype),
            pltpu.VMEM((slots, BLK, BLK), jnp.float32),
            pltpu.SemaphoreType.DMA((depth,)),
            pltpu.SemaphoreType.DMA((depth,)),
            pltpu.SemaphoreType.DMA((slots,)),
            pltpu.SemaphoreType.DMA((slots,)),
        ],
        input_output_aliases={4: 0, 5: 1},
        compiler_params=pltpu.CompilerParams(vmem_limit_bytes=room),
        cost_estimate=pl.CostEstimate(
            flops=slots * tokens * BLK * BLK,
            bytes_accessed=slots * tokens * BLK * 4,
            transcendentals=0,
        ),
        name="products_here",
    )(jobs, sizes, activations, out_grad, *partial)


def hosted_kernel(host_ref, act_ref, cols_ref, tiles_ref, row_buf, sems):
    def row_copy(n):
        source = column(act_ref, jnp.maximum(host_ref[2 + n], 0))
        return pltpu.make_async_copy(source, row_buf.at[n], sems.at[n])

    pl.loop(0, 2)(lambda n: row_copy(n).start())

    @pl.loop(0, 2)
    def _(n):
        row_copy(n).wait()
        tiles_ref[n] = multiply(row_buf[n], cols_ref[n])


def products_hosted(host, activations, cols):
    tokens = activations.shape[0]
    return pl.pallas_call(
        hosted_kernel,
        out_shape=jax.ShapeDtypeStruct((2, BLK, BLK), jnp.float32),
        in_specs=[SCALARS, ANYWHERE, IN_VMEM],
        out_specs=IN_VMEM,
        scratch_shapes=[
            pltpu.VMEM((2, tokens, BLK), activations.dtype),
            pltpu.SemaphoreType.DMA((2,)),
        ],
        compiler_params=pltpu.CompilerParams(vmem_limit_bytes=4 * MIB),
        cost_estimate=pl.CostEstimate(
            flops=4 * tokens * BLK * BLK, bytes_accessed=8 * tokens * BLK, transcendentals=0
        ),
        name="products_hosted",
    )(host, activations, cols)


def moved_kernel(shift, first, job_ref, size_ref, rows_ref, cols_ref, *rest):
    *back_refs, _, _, keep_ref, send_ref, stage, out_sems = rest
    slots = cols_ref.shape[0]
    out = functools.partial(out_copy, stage, keep_ref, send_ref, out_sems)
    before = jnp.int32(0)
    for earlier in range(1, shift):
        before = before + size_ref[earlier]

    def each_job(act):
        @pl.loop(0, size_ref[shift])
        def _(job):
            base = 3 * (shift * slots + job)
            block = job_ref[base + 1] - first

            @pl.when((block >= 0) & (block < rows_ref.shape[0]))
            def _():
                act(job, job_ref[base], block)

    def work(job, place, block):
        stage[place] = multiply(rows_ref[block], cols_ref[before + job])
        out(place, begin)

    def each_back(act):
        for back_ref in back_refs:

            @pl.loop(0, 2)
            def _(n):
                place = size_ref[size_ref.shape[0] - 2 + n]

                @pl.when(place >= 0)
                def _():
                    out_copy(back_ref, keep_ref, send_ref, out_sems, place, act, n)

    each_back(begin)
    each_job(work)
    each_job(lambda _, place, __: out(place, finish))
    each_back(finish)


def products_moved(shift, first, jobs, sizes, rows, cols, partial, back=()):
    slots, tokens = cols.shape[:2]
    half = jax.ShapeDtypeStruct((slots // 2, BLK, BLK), jnp.float32)
    room = (rows.shape[0] + slots) * tokens * BLK * 2 + slots * BLK * BLK * 4 + 4 * MIB
    return pl.pallas_call(
        functools.partial(moved_kernel, shift, first),
        out_shape=(half, half),
        in_specs=[SCALARS] * 2 + [IN_VMEM] * 2 + [ANYWHERE] * (2 + len(back)),
        out_specs=(ANYWHERE,) * 2,
        scratch_shapes=[
            pltpu.VMEM((slots, BLK, BLK), jnp.float32),
            pltpu.SemaphoreType.DMA((slots,)),
        ],
        input_output_aliases={4 + len(back): 0, 5 + len(back): 1},
        compiler_params=pltpu.CompilerParams(vmem_limit_bytes=room),
        cost_estimate=pl.CostEstimate(
            flops=slots * tokens * BLK * BLK,
            bytes_accessed=slots * tokens * BLK * 4,
            transcendentals=0,
        ),
        name="products_moved",
    )(jobs, sizes, rows, cols, *back, *partial)


def reduce_to_owner(owners, keep, send):
    lanes = (keep.shape[0] + send.shape[0]) // owners
    steps = owners.bit_length() - 1

    def swap(part, mask):
        return lax.ppermute(part, "dp", [(d, d ^ mask) for d in range(owners)])

    def halve(part, i):
        middle = part[0].shape[0] // 2
        arrived = swap(part[1], 1 << i)
        return [part[0][:middle] + arrived[:middle], part[0][middle:] + arrived[middle:]]

    if steps < 4:
        part = [keep, send]
        for i in range(steps - 1):
            part = halve(part, i)
        return part[0] + swap(part[1], 1 << (steps - 1))

    part = [keep, send]
    for i in range(steps - 4):
        part = halve(part, i)
    keep = part[0]
    came = swap(part[1], 1 << (steps - 4))

    def chunk(first):
        held = slice(first * lanes, (first + 2) * lanes)
        sent = slice((first + 4) * lanes, (first + 6) * lanes)
        return keep[held] + came[held], swap(keep[sent] + came[sent], 1 << (steps - 3))

    far_keep, far_came = chunk(2)
    near_keep, near_came = chunk(0)
    low, high = 1 << (steps - 2), 1 << (steps - 1)
    both_came = swap(far_keep[lanes:] + far_came[lanes:], low | high)
    low_came = swap(far_keep[:lanes] + far_came[:lanes], low)
    high_came = swap(near_keep[lanes:] + near_came[lanes:], high)
    return near_keep[:lanes] + near_came[:lanes] + both_came + low_came + high_came


def on_device(shards, owners, activations, out_grad, tile_list, tile_count):
    slots = tile_list.shape[1]
    row_blocks = activations.shape[1] // BLK
    col_blocks = out_grad.shape[1] // BLK

    slot_list = jnp.concatenate([tile_list[0, :, 0], tile_list[0, :, 1], tile_count])
    routes = [[(i, (i + s) % shards) for i in range(shards)] for s in range(shards)]
    lists = [slot_list] + [lax.ppermute(slot_list, "mp", routes[s]) for s in range(1, shards)]
    limit = min(row_blocks, slots)
    sizes = [n for n in (3, 4, 5, 6, 7, 8, 9, 10, 12) if n < limit] + [limit]
    hosted_sizes = [n for n in (3, 4, 5, 6, 7) if shards == 2 and n < limit]
    branch, send, host = make_plan(shards, row_blocks, col_blocks, sizes, hosted_sizes, lists)
    kinds = [(n, False) for n in sizes] + [(n, True) for n in hosted_sizes]

    carried = ()
    for shift in range(1, shards):

        def move(count, hosted, send, host, slot_list, carried, activations, out_grad):
            cut = [count - 1, 1]
            mixed = [out_grad] if hosted else []
            packed = pack(shift, row_blocks, cut, send, activations, *mixed)
            arrived = [lax.ppermute(part, "mp", routes[shift]) for part in packed]
            jobs, amounts = make_jobs(shards, owners, row_blocks, col_blocks, slot_list, host)
            if shift == 1:
                blank = jnp.zeros((slots // 2, BLK, BLK), jnp.float32)
                blank = lax.optimization_barrier((blank, blank))
                *partial, later = products_here(
                    shards, slots, jobs, amounts, activations, out_grad, blank
                )
            else:
                *partial, later = carried
            back = []
            if hosted:
                host, partial = lax.optimization_barrier((host, partial))
                tiles = products_hosted(host, activations, arrived[0])
                tiles, partial = lax.optimization_barrier((tiles, partial))
                back = [lax.ppermute(tiles, "mp", routes[shift])]
            for n, rows in enumerate(arrived):
                last = n + 1 == len(arrived)
                partial = products_moved(
                    shift, sum(cut[:n]), jobs, amounts, rows, later, partial, back if last else ()
                )
            if shift + 1 < shards:
                return *partial, later
            return reduce_to_owner(owners, *partial)[None]

        carried = lax.switch(
            branch[shift - 1],
            [functools.partial(move, count, hosted) for count, hosted in kinds],
            send,
            host,
            slot_list,
            carried,
            activations,
            out_grad,
        )
    return carried


def solution(mesh):
    placed = (P("dp", "mp"), P("dp", "mp"), P("mp", None, None), P("mp"))
    return jax.shard_map(
        functools.partial(on_device, mesh.shape["mp"], mesh.shape["dp"]),
        mesh=mesh,
        in_specs=placed,
        out_specs=P("mp", "dp", None, None),
        check_vma=False,
    )
```

```python
import functools

import jax
import jax.numpy as jnp
from jax import lax
from jax.experimental import pallas as pl
from jax.experimental.pallas import tpu as pltpu
from jax.sharding import PartitionSpec as P

BLK = 128
MIB = 1024 * 1024
SCALARS = pl.BlockSpec(memory_space=pltpu.SMEM)
ANYWHERE = pl.BlockSpec(memory_space=pl.ANY)
IN_VMEM = pl.BlockSpec(memory_space=pltpu.VMEM)


def skip(*_):
    pass


def scan(slots, row_blocks, origin, list_ref, note=skip, without=(), first=0):
    def step(k, state):
        count, once, twice = state
        block = list_ref[k] - origin * row_blocks
        wanted = (k < list_ref[2 * slots]) & (block >= 0) & (block < row_blocks)
        for other in without:
            wanted = wanted & (k != other)
        bit = jnp.where(wanted, jnp.int32(1) << (block & 31), 0)
        new = ((once & bit) == 0) & wanted
        note(jnp.where(new, count, row_blocks), block)
        return count + new.astype(jnp.int32), once | bit, twice | (once & bit)

    state = jnp.int32(first), jnp.int32(0), jnp.int32(0)
    return lax.fori_loop(0, slots, step, state, unroll=slots <= 16)


def plan_kernel(shards, row_blocks, sizes, *refs):
    lists, (branch_ref, send_ref, host_ref) = refs[:shards], refs[shards:]
    slots = (lists[0].shape[0] - 1) // 2
    me = lax.axis_index("mp")
    for n in range(5):
        host_ref[n] = -1 if n < 4 else 0
    for shift in range(1, shards):
        for b in range(row_blocks):
            send_ref[(shift - 1) * (row_blocks + 1) + b] = 0

        def note_block(place, block):
            send_ref[(shift - 1) * (row_blocks + 1) + place] = block

        most = jnp.int32(0)
        for s in range(shards):
            origin = lax.rem(me - s - shift + 2 * shards, shards)
            note = note_block if s == shards - shift else skip
            most = jnp.maximum(most, scan(slots, row_blocks, origin, lists[s], note)[0])
        branch_ref[shift - 1] = sum((most > size).astype(jnp.int32) for size in sizes[:-1])


def pair_plan_kernel(row_blocks, col_blocks, sizes, hosted_sizes, *refs):
    mine_ref, theirs_ref, branch_ref, send_ref, host_ref = refs
    slots = (mine_ref.shape[0] - 1) // 2
    me = lax.axis_index("mp")
    my_need, my_once, my_twice = scan(slots, row_blocks, 1 - me, mine_ref)
    for b in range(row_blocks):
        send_ref[b] = 0
    their_need, their_once, their_twice = scan(slots, row_blocks, me, theirs_ref)
    i_am_heavy = my_need > their_need
    heavy, light = jnp.maximum(my_need, their_need), jnp.minimum(my_need, their_need)
    single = jnp.where(i_am_heavy, my_once & ~my_twice, their_once & ~their_twice)
    singles = sum((single >> b) & 1 for b in range(row_blocks))

    best, hosted, height = 4 * heavy, jnp.int32(0), heavy
    for count in (1, 2):
        level = jnp.maximum(jnp.maximum(heavy - count, light + count), hosted_sizes[0])
        cost = 4 * level + 2
        better = (singles >= count) & (level <= hosted_sizes[-1]) & (cost < best)
        best = jnp.where(better, cost, best)
        hosted = jnp.where(better, count, hosted)
        height = jnp.where(better, level, height)
    plain = sum((height > size).astype(jnp.int32) for size in sizes[:-1])
    shared = sum((height > size).astype(jnp.int32) for size in hosted_sizes[:-1])
    branch_ref[0] = jnp.where(hosted > 0, len(sizes) + shared, plain)

    def pick(k, state):
        found, one, two = state
        block = jnp.where(i_am_heavy, mine_ref[k], theirs_ref[k])
        block = block - jnp.where(i_am_heavy, 1 - me, me) * row_blocks
        live = k < jnp.where(i_am_heavy, mine_ref[2 * slots], theirs_ref[2 * slots])
        fits = live & (block >= 0) & (block < row_blocks) & (found < hosted)
        fits = fits & (((single >> (block & 31)) & 1) > 0)
        one = jnp.where(fits & (found == 0), k, one)
        two = jnp.where(fits & (found == 1), k, two)
        return found + fits.astype(jnp.int32), one, two

    state = jnp.int32(0), jnp.int32(-1), jnp.int32(-1)
    _, *picks = lax.fori_loop(0, slots, pick, state, unroll=slots <= 16)
    my_picks = [jnp.where(i_am_heavy, k, -1) for k in picks]
    their_picks = [jnp.where(i_am_heavy, -1, k) for k in picks]
    for n in range(2):
        host_ref[n] = my_picks[n]
        row = theirs_ref[jnp.maximum(their_picks[n], 0)] - me * row_blocks
        host_ref[2 + n] = jnp.where(their_picks[n] >= 0, row, -1)
        col = mine_ref[slots + jnp.maximum(my_picks[n], 0)] - me * col_blocks
        send_ref[jnp.where(my_picks[n] >= 0, n, row_blocks)] = row_blocks + col
    host_ref[4] = jnp.where(i_am_heavy, 0, hosted)

    def note_block(place, block):
        send_ref[place] = block

    ahead = jnp.where(i_am_heavy, hosted, 0)
    scan(slots, row_blocks, me, theirs_ref, note_block, their_picks, ahead)


def make_plan(shards, row_blocks, col_blocks, sizes, hosted_sizes, lists):
    kernel = functools.partial(plan_kernel, shards, row_blocks, sizes)
    if hosted_sizes:
        kernel = functools.partial(pair_plan_kernel, row_blocks, col_blocks, sizes, hosted_sizes)
    return pl.pallas_call(
        kernel,
        out_shape=(
            jax.ShapeDtypeStruct((shards - 1,), jnp.int32),
            jax.ShapeDtypeStruct(((shards - 1) * (row_blocks + 1),), jnp.int32),
            jax.ShapeDtypeStruct((5,), jnp.int32),
        ),
        in_specs=[SCALARS] * shards,
        out_specs=(SCALARS,) * 3,
        name="plan",
    )(*lists)


def jobs_kernel(shards, owners, row_blocks, col_blocks, list_ref, host_ref, job_ref, size_ref, seen):
    slots = (list_ref.shape[0] - 1) // 2
    lanes = slots // owners
    steps = owners.bit_length() - 1
    me = lax.axis_index("dp")
    shard = lax.axis_index("mp")

    def place_of(k):
        relative = (k // lanes) ^ me
        place = jnp.int32(0)
        for i in range(steps):
            place = place | (((relative >> i) & 1) << (steps - 1 - i))
        return place * lanes + k % lanes

    for n in range(2):
        slot = host_ref[n]
        size_ref[shards + n] = jnp.where(slot >= 0, place_of(jnp.maximum(slot, 0)), -1)
    for shift in range(shards):
        base = shift * slots * 3
        size_ref[shift] = 0
        origin = lax.rem(shard + shards - shift, shards)
        first = host_ref[4] if shift else 0
        if shift:
            for b in range(row_blocks):
                seen[b] = -1

        def step(k, count):
            block = list_ref[k] - origin * row_blocks
            wanted = (block >= 0) & (block < row_blocks)
            wanted = wanted & (k != host_ref[0]) & (k != host_ref[1])

            @pl.when(wanted)
            def _():
                source = block
                if shift:
                    known = seen[block]
                    source = jnp.where(known < 0, count, known)
                    seen[block] = source
                job = size_ref[shift]
                job_ref[base + 3 * job] = place_of(k)
                job_ref[base + 3 * job + 1] = source
                job_ref[base + 3 * job + 2] = list_ref[slots + k] - shard * col_blocks
                size_ref[shift] = job + 1

            at = jnp.clip(block, 0, row_blocks - 1)
            return jnp.where(wanted, jnp.maximum(count, seen[at] + 1), count)

        lax.fori_loop(0, list_ref[2 * slots], step, first)


def make_jobs(shards, owners, row_blocks, col_blocks, slot_list, host):
    slots = (slot_list.shape[0] - 1) // 2
    return pl.pallas_call(
        functools.partial(jobs_kernel, shards, owners, row_blocks, col_blocks),
        out_shape=(
            jax.ShapeDtypeStruct((shards * slots * 3,), jnp.int32),
            jax.ShapeDtypeStruct((shards + 2,), jnp.int32),
        ),
        in_specs=[SCALARS] * 2,
        out_specs=(SCALARS,) * 2,
        scratch_shapes=[pltpu.SMEM((row_blocks,), jnp.int32)],
        cost_estimate=pl.CostEstimate(flops=0, bytes_accessed=1 << 20, transcendentals=0),
        name="jobs",
    )(slot_list, host)


def pack_kernel(shift, row_blocks, mixed, send_ref, act_ref, *rest):
    *out_refs, buf, in_sems, out_sems = rest[1:] if mixed else rest
    count = buf.shape[0]

    @pl.loop(0, count)
    def _(j):
        block = send_ref[(shift - 1) * (row_blocks + 1) + j]

        def fetch(source):
            pltpu.make_async_copy(source, buf.at[j], in_sems.at[j]).start()

        if mixed:
            pl.when(block < row_blocks)(lambda: fetch(column(act_ref, block)))
            pl.when(block >= row_blocks)(lambda: fetch(column(rest[0], block - row_blocks)))
        else:
            fetch(column(act_ref, block))

    def each_out(act):
        first = 0
        for out_ref in out_refs:

            @pl.loop(0, out_ref.shape[0])
            def _(j):
                at = first + j
                act(at, pltpu.make_async_copy(buf.at[at], out_ref.at[j], out_sems.at[at]))

            first += out_ref.shape[0]

    def pass_on(at, copy):
        pltpu.make_async_copy(column(act_ref, 0), buf.at[at], in_sems.at[at]).wait()
        copy.start()

    each_out(pass_on)
    each_out(lambda _, copy: copy.wait())


def pack(shift, row_blocks, sizes, send, activations, *out_grad):
    tokens = activations.shape[0]
    count = sum(sizes)
    return pl.pallas_call(
        functools.partial(pack_kernel, shift, row_blocks, bool(out_grad)),
        out_shape=tuple(
            jax.ShapeDtypeStruct((size, tokens, BLK), activations.dtype) for size in sizes
        ),
        in_specs=[SCALARS] + [ANYWHERE] * (1 + len(out_grad)),
        out_specs=(ANYWHERE,) * len(sizes),
        scratch_shapes=[
            pltpu.VMEM((count, tokens, BLK), activations.dtype),
            pltpu.SemaphoreType.DMA((count,)),
            pltpu.SemaphoreType.DMA((count,)),
        ],
        compiler_params=pltpu.CompilerParams(
            vmem_limit_bytes=count * tokens * BLK * 2 + 2 * MIB
        ),
        cost_estimate=pl.CostEstimate(
            flops=0, bytes_accessed=count * tokens * BLK * 4, transcendentals=0
        ),
        name="pack",
    )(send, activations, *out_grad)


def multiply(rows, cols):
    return lax.dot_general(
        rows, cols, (((0,), (0,)), ((), ())), preferred_element_type=jnp.float32
    )


def column(ref, block):
    return ref.at[:, pl.ds(pl.multiple_of(block * BLK, BLK), BLK)]


def out_copy(stage, keep_ref, send_ref, sems, place, act, at=None):
    half = keep_ref.shape[0]
    at = place if at is None else at

    @pl.when(place < half)
    def _():
        act(pltpu.make_async_copy(stage.at[at], keep_ref.at[place], sems.at[place]))

    @pl.when(place >= half)
    def _():
        act(pltpu.make_async_copy(stage.at[at], send_ref.at[place - half], sems.at[place]))


def begin(copy):
    copy.start()


def finish(copy):
    copy.wait()


def here_kernel(shards, job_ref, size_ref, act_ref, grad_ref, *rest):
    _, _, keep_ref, send_ref, later_ref, row_buf, col_buf, stage, *sems = rest
    row_sems, col_sems, later_sems, out_sems = sems
    slots = later_ref.shape[0]
    depth = col_buf.shape[0]
    jobs = size_ref[0]
    out = functools.partial(out_copy, stage, keep_ref, send_ref, out_sems)

    def row_copy(job):
        at = lax.rem(job, depth)
        source = column(act_ref, job_ref[3 * job + 1])
        return pltpu.make_async_copy(source, row_buf.at[at], row_sems.at[at])

    def col_copy(job):
        at = lax.rem(job, depth)
        source = column(grad_ref, job_ref[3 * job + 2])
        return pltpu.make_async_copy(source, col_buf.at[at], col_sems.at[at])

    def each_later(act):
        before = jnp.int32(0)
        for shift in range(1, shards):

            @pl.loop(0, size_ref[shift])
            def _(job):
                source = column(grad_ref, job_ref[3 * (shift * slots + job) + 2])
                at = before + job
                act(pltpu.make_async_copy(source, later_ref.at[at], later_sems.at[at]))

            before = before + size_ref[shift]

    def start(job):
        row_copy(job).start()
        col_copy(job).start()

    pl.loop(0, jnp.minimum(depth, jobs))(start)
    each_later(begin)

    @pl.loop(0, jobs)
    def _(job):
        at = lax.rem(job, depth)
        place = job_ref[3 * job]
        row_copy(job).wait()
        col_copy(job).wait()
        stage[place] = multiply(row_buf[at], col_buf[at])
        out(place, begin)
        if depth < slots:
            pl.when(job + depth < jobs)(lambda: start(job + depth))

    each_later(finish)

    @pl.loop(0, jobs)
    def _(job):
        out(job_ref[3 * job], finish)


def products_here(shards, slots, jobs, sizes, activations, out_grad, partial):
    tokens = out_grad.shape[0]
    depth = min(slots, 8)
    half = jax.ShapeDtypeStruct((slots // 2, BLK, BLK), jnp.float32)
    room = 2 * depth * tokens * BLK * 2 + slots * BLK * BLK * 4 + 4 * MIB
    return pl.pallas_call(
        functools.partial(here_kernel, shards),
        out_shape=(half, half, jax.ShapeDtypeStruct((slots, tokens, BLK), out_grad.dtype)),
        in_specs=[SCALARS] * 2 + [ANYWHERE] * 4,
        out_specs=(ANYWHERE,) * 3,
        scratch_shapes=[
            pltpu.VMEM((depth, tokens, BLK), activations.dtype),
            pltpu.VMEM((depth, tokens, BLK), out_grad.dtype),
            pltpu.VMEM((slots, BLK, BLK), jnp.float32),
            pltpu.SemaphoreType.DMA((depth,)),
            pltpu.SemaphoreType.DMA((depth,)),
            pltpu.SemaphoreType.DMA((slots,)),
            pltpu.SemaphoreType.DMA((slots,)),
        ],
        input_output_aliases={4: 0, 5: 1},
        compiler_params=pltpu.CompilerParams(vmem_limit_bytes=room),
        cost_estimate=pl.CostEstimate(
            flops=slots * tokens * BLK * BLK,
            bytes_accessed=slots * tokens * BLK * 4,
            transcendentals=0,
        ),
        name="products_here",
    )(jobs, sizes, activations, out_grad, *partial)


def hosted_kernel(host_ref, act_ref, cols_ref, tiles_ref, row_buf, sems):
    def row_copy(n):
        source = column(act_ref, jnp.maximum(host_ref[2 + n], 0))
        return pltpu.make_async_copy(source, row_buf.at[n], sems.at[n])

    pl.loop(0, 2)(lambda n: row_copy(n).start())

    @pl.loop(0, 2)
    def _(n):
        row_copy(n).wait()
        tiles_ref[n] = multiply(row_buf[n], cols_ref[n])


def products_hosted(host, activations, cols):
    tokens = activations.shape[0]
    return pl.pallas_call(
        hosted_kernel,
        out_shape=jax.ShapeDtypeStruct((2, BLK, BLK), jnp.float32),
        in_specs=[SCALARS, ANYWHERE, IN_VMEM],
        out_specs=IN_VMEM,
        scratch_shapes=[
            pltpu.VMEM((2, tokens, BLK), activations.dtype),
            pltpu.SemaphoreType.DMA((2,)),
        ],
        compiler_params=pltpu.CompilerParams(vmem_limit_bytes=4 * MIB),
        cost_estimate=pl.CostEstimate(
            flops=4 * tokens * BLK * BLK, bytes_accessed=8 * tokens * BLK, transcendentals=0
        ),
        name="products_hosted",
    )(host, activations, cols)


def moved_kernel(shift, first, job_ref, size_ref, rows_ref, cols_ref, *rest):
    *back_refs, _, _, keep_ref, send_ref, stage, out_sems = rest
    slots = cols_ref.shape[0]
    out = functools.partial(out_copy, stage, keep_ref, send_ref, out_sems)
    before = jnp.int32(0)
    for earlier in range(1, shift):
        before = before + size_ref[earlier]

    def each_job(act):
        @pl.loop(0, size_ref[shift])
        def _(job):
            base = 3 * (shift * slots + job)
            block = job_ref[base + 1] - first

            @pl.when((block >= 0) & (block < rows_ref.shape[0]))
            def _():
                act(job, job_ref[base], block)

    def work(job, place, block):
        stage[place] = multiply(rows_ref[block], cols_ref[before + job])
        out(place, begin)

    def each_back(act):
        for back_ref in back_refs:

            @pl.loop(0, 2)
            def _(n):
                place = size_ref[size_ref.shape[0] - 2 + n]

                @pl.when(place >= 0)
                def _():
                    out_copy(back_ref, keep_ref, send_ref, out_sems, place, act, n)

    each_back(begin)
    each_job(work)
    each_job(lambda _, place, __: out(place, finish))
    each_back(finish)


def products_moved(shift, first, jobs, sizes, rows, cols, partial, back=()):
    slots, tokens = cols.shape[:2]
    half = jax.ShapeDtypeStruct((slots // 2, BLK, BLK), jnp.float32)
    room = (rows.shape[0] + slots) * tokens * BLK * 2 + slots * BLK * BLK * 4 + 4 * MIB
    return pl.pallas_call(
        functools.partial(moved_kernel, shift, first),
        out_shape=(half, half),
        in_specs=[SCALARS] * 2 + [IN_VMEM] * 2 + [ANYWHERE] * (2 + len(back)),
        out_specs=(ANYWHERE,) * 2,
        scratch_shapes=[
            pltpu.VMEM((slots, BLK, BLK), jnp.float32),
            pltpu.SemaphoreType.DMA((slots,)),
        ],
        input_output_aliases={4 + len(back): 0, 5 + len(back): 1},
        compiler_params=pltpu.CompilerParams(vmem_limit_bytes=room),
        cost_estimate=pl.CostEstimate(
            flops=slots * tokens * BLK * BLK,
            bytes_accessed=slots * tokens * BLK * 4,
            transcendentals=0,
        ),
        name="products_moved",
    )(jobs, sizes, rows, cols, *back, *partial)


def reduce_to_owner(owners, keep, send):
    lanes = (keep.shape[0] + send.shape[0]) // owners
    steps = owners.bit_length() - 1

    def swap(part, mask):
        return lax.ppermute(part, "dp", [(d, d ^ mask) for d in range(owners)])

    def halve(part, i):
        middle = part[0].shape[0] // 2
        arrived = swap(part[1], 1 << i)
        return [part[0][:middle] + arrived[:middle], part[0][middle:] + arrived[middle:]]

    if steps < 4:
        part = [keep, send]
        for i in range(steps - 1):
            part = halve(part, i)
        return part[0] + swap(part[1], 1 << (steps - 1))

    part = [keep, send]
    for i in range(steps - 4):
        part = halve(part, i)
    keep = part[0]
    came = swap(part[1], 1 << (steps - 4))

    def chunk(first):
        held = slice(first * lanes, (first + 2) * lanes)
        sent = slice((first + 4) * lanes, (first + 6) * lanes)
        return keep[held] + came[held], swap(keep[sent] + came[sent], 1 << (steps - 3))

    far_keep, far_came = chunk(2)
    near_keep, near_came = chunk(0)
    low, high = 1 << (steps - 2), 1 << (steps - 1)
    both_came = swap(far_keep[lanes:] + far_came[lanes:], low | high)
    low_came = swap(far_keep[:lanes] + far_came[:lanes], low)
    high_came = swap(near_keep[lanes:] + near_came[lanes:], high)
    return near_keep[:lanes] + near_came[:lanes] + both_came + low_came + high_came


def on_device(shards, owners, activations, out_grad, tile_list, tile_count):
    slots = tile_list.shape[1]
    row_blocks = activations.shape[1] // BLK
    col_blocks = out_grad.shape[1] // BLK

    slot_list = jnp.concatenate([tile_list[0, :, 0], tile_list[0, :, 1], tile_count])
    routes = [[(i, (i + s) % shards) for i in range(shards)] for s in range(shards)]
    lists = [slot_list] + [lax.ppermute(slot_list, "mp", routes[s]) for s in range(1, shards)]
    limit = min(row_blocks, slots)
    sizes = [n for n in (3, 4, 5, 6, 7, 8, 9, 10, 12) if n < limit] + [limit]
    hosted_sizes = [n for n in (3, 4, 5, 6, 7) if shards == 2 and n < limit]
    branch, send, host = make_plan(shards, row_blocks, col_blocks, sizes, hosted_sizes, lists)
    kinds = [(n, False) for n in sizes] + [(n, True) for n in hosted_sizes]

    carried = ()
    for shift in range(1, shards):

        def move(count, hosted, send, host, slot_list, carried, activations, out_grad):
            cut = [count - 1, 1]
            mixed = [out_grad] if hosted else []
            packed = pack(shift, row_blocks, cut, send, activations, *mixed)
            arrived = [lax.ppermute(part, "mp", routes[shift]) for part in packed]
            jobs, amounts = make_jobs(shards, owners, row_blocks, col_blocks, slot_list, host)
            if shift == 1:
                blank = jnp.zeros((slots // 2, BLK, BLK), jnp.float32)
                blank = lax.optimization_barrier((blank, blank))
                *partial, later = products_here(
                    shards, slots, jobs, amounts, activations, out_grad, blank
                )
            else:
                *partial, later = carried
            back = []
            if hosted:
                host, partial = lax.optimization_barrier((host, partial))
                tiles = products_hosted(host, activations, arrived[0])
                tiles, partial = lax.optimization_barrier((tiles, partial))
                back = [lax.ppermute(tiles, "mp", routes[shift])]
            for n, rows in enumerate(arrived):
                last = n + 1 == len(arrived)
                partial = products_moved(
                    shift, sum(cut[:n]), jobs, amounts, rows, later, partial, back if last else ()
                )
            if shift + 1 < shards:
                return *partial, later
            return reduce_to_owner(owners, *partial)[None]

        carried = lax.switch(
            branch[shift - 1],
            [functools.partial(move, count, hosted) for count, hosted in kinds],
            send,
            host,
            slot_list,
            carried,
            activations,
            out_grad,
        )
    return carried


def solution(mesh):
    placed = (P("dp", "mp"), P("dp", "mp"), P("mp", None, None), P("mp"))
    return jax.shard_map(
        functools.partial(on_device, mesh.shape["mp"], mesh.shape["dp"]),
        mesh=mesh,
        in_specs=placed,
        out_specs=P("mp", "dp", None, None),
        check_vma=False,
    )
```

```python
import functools

import jax
import jax.numpy as jnp
from jax import lax
from jax.experimental import pallas as pl
from jax.experimental.pallas import tpu as pltpu
from jax.sharding import PartitionSpec as P

BLK = 128
MIB = 1024 * 1024
SCALARS = pl.BlockSpec(memory_space=pltpu.SMEM)
ANYWHERE = pl.BlockSpec(memory_space=pl.ANY)
IN_VMEM = pl.BlockSpec(memory_space=pltpu.VMEM)


def skip(*_):
    pass


def scan(slots, row_blocks, origin, list_ref, note=skip, without=(), first=0):
    def step(k, state):
        count, once, twice = state
        block = list_ref[k] - origin * row_blocks
        wanted = (k < list_ref[2 * slots]) & (block >= 0) & (block < row_blocks)
        for other in without:
            wanted = wanted & (k != other)
        bit = jnp.where(wanted, jnp.int32(1) << (block & 31), 0)
        new = ((once & bit) == 0) & wanted
        note(jnp.where(new, count, row_blocks), block)
        return count + new.astype(jnp.int32), once | bit, twice | (once & bit)

    state = jnp.int32(first), jnp.int32(0), jnp.int32(0)
    return lax.fori_loop(0, slots, step, state, unroll=slots <= 16)


def plan_kernel(shards, row_blocks, sizes, *refs):
    lists, (branch_ref, send_ref, host_ref) = refs[:shards], refs[shards:]
    slots = (lists[0].shape[0] - 1) // 2
    me = lax.axis_index("mp")
    for n in range(5):
        host_ref[n] = -1 if n < 4 else 0
    for shift in range(1, shards):
        for b in range(row_blocks):
            send_ref[(shift - 1) * (row_blocks + 1) + b] = 0

        def note_block(place, block):
            send_ref[(shift - 1) * (row_blocks + 1) + place] = block

        most = jnp.int32(0)
        for s in range(shards):
            origin = lax.rem(me - s - shift + 2 * shards, shards)
            note = note_block if s == shards - shift else skip
            most = jnp.maximum(most, scan(slots, row_blocks, origin, lists[s], note)[0])
        branch_ref[shift - 1] = sum((most > size).astype(jnp.int32) for size in sizes[:-1])


def pair_plan_kernel(row_blocks, col_blocks, sizes, hosted_sizes, *refs):
    mine_ref, theirs_ref, branch_ref, send_ref, host_ref = refs
    slots = (mine_ref.shape[0] - 1) // 2
    me = lax.axis_index("mp")
    my_need, my_once, my_twice = scan(slots, row_blocks, 1 - me, mine_ref)
    for b in range(row_blocks):
        send_ref[b] = 0
    their_need, their_once, their_twice = scan(slots, row_blocks, me, theirs_ref)
    i_am_heavy = my_need > their_need
    heavy, light = jnp.maximum(my_need, their_need), jnp.minimum(my_need, their_need)
    single = jnp.where(i_am_heavy, my_once & ~my_twice, their_once & ~their_twice)
    singles = sum((single >> b) & 1 for b in range(row_blocks))

    best, hosted, height = 4 * heavy, jnp.int32(0), heavy
    for count in (1, 2):
        level = jnp.maximum(jnp.maximum(heavy - count, light + count), hosted_sizes[0])
        cost = 4 * level + 2
        better = (singles >= count) & (level <= hosted_sizes[-1]) & (cost < best)
        best = jnp.where(better, cost, best)
        hosted = jnp.where(better, count, hosted)
        height = jnp.where(better, level, height)
    plain = sum((height > size).astype(jnp.int32) for size in sizes[:-1])
    shared = sum((height > size).astype(jnp.int32) for size in hosted_sizes[:-1])
    branch_ref[0] = jnp.where(hosted > 0, len(sizes) + shared, plain)

    def pick(k, state):
        found, one, two = state
        block = jnp.where(i_am_heavy, mine_ref[k], theirs_ref[k])
        block = block - jnp.where(i_am_heavy, 1 - me, me) * row_blocks
        live = k < jnp.where(i_am_heavy, mine_ref[2 * slots], theirs_ref[2 * slots])
        fits = live & (block >= 0) & (block < row_blocks) & (found < hosted)
        fits = fits & (((single >> (block & 31)) & 1) > 0)
        one = jnp.where(fits & (found == 0), k, one)
        two = jnp.where(fits & (found == 1), k, two)
        return found + fits.astype(jnp.int32), one, two

    state = jnp.int32(0), jnp.int32(-1), jnp.int32(-1)
    _, *picks = lax.fori_loop(0, slots, pick, state, unroll=slots <= 16)
    my_picks = [jnp.where(i_am_heavy, k, -1) for k in picks]
    their_picks = [jnp.where(i_am_heavy, -1, k) for k in picks]
    for n in range(2):
        host_ref[n] = my_picks[n]
        row = theirs_ref[jnp.maximum(their_picks[n], 0)] - me * row_blocks
        host_ref[2 + n] = jnp.where(their_picks[n] >= 0, row, -1)
        col = mine_ref[slots + jnp.maximum(my_picks[n], 0)] - me * col_blocks
        send_ref[jnp.where(my_picks[n] >= 0, n, row_blocks)] = row_blocks + col
    host_ref[4] = jnp.where(i_am_heavy, 0, hosted)

    def note_block(place, block):
        send_ref[place] = block

    ahead = jnp.where(i_am_heavy, hosted, 0)
    scan(slots, row_blocks, me, theirs_ref, note_block, their_picks, ahead)


def make_plan(shards, row_blocks, col_blocks, sizes, hosted_sizes, lists):
    kernel = functools.partial(plan_kernel, shards, row_blocks, sizes)
    if hosted_sizes:
        kernel = functools.partial(pair_plan_kernel, row_blocks, col_blocks, sizes, hosted_sizes)
    return pl.pallas_call(
        kernel,
        out_shape=(
            jax.ShapeDtypeStruct((shards - 1,), jnp.int32),
            jax.ShapeDtypeStruct(((shards - 1) * (row_blocks + 1),), jnp.int32),
            jax.ShapeDtypeStruct((5,), jnp.int32),
        ),
        in_specs=[SCALARS] * shards,
        out_specs=(SCALARS,) * 3,
        name="plan",
    )(*lists)


def jobs_kernel(shards, owners, row_blocks, col_blocks, list_ref, host_ref, job_ref, size_ref, seen):
    slots = (list_ref.shape[0] - 1) // 2
    lanes = slots // owners
    steps = owners.bit_length() - 1
    me = lax.axis_index("dp")
    shard = lax.axis_index("mp")

    def place_of(k):
        relative = (k // lanes) ^ me
        place = jnp.int32(0)
        for i in range(steps):
            place = place | (((relative >> i) & 1) << (steps - 1 - i))
        return place * lanes + k % lanes

    for n in range(2):
        slot = host_ref[n]
        size_ref[shards + n] = jnp.where(slot >= 0, place_of(jnp.maximum(slot, 0)), -1)
    for shift in range(shards):
        base = shift * slots * 3
        size_ref[shift] = 0
        origin = lax.rem(shard + shards - shift, shards)
        first = host_ref[4] if shift else 0
        if shift:
            for b in range(row_blocks):
                seen[b] = -1

        def step(k, count):
            block = list_ref[k] - origin * row_blocks
            wanted = (block >= 0) & (block < row_blocks)
            wanted = wanted & (k != host_ref[0]) & (k != host_ref[1])

            @pl.when(wanted)
            def _():
                source = block
                if shift:
                    known = seen[block]
                    source = jnp.where(known < 0, count, known)
                    seen[block] = source
                job = size_ref[shift]
                job_ref[base + 3 * job] = place_of(k)
                job_ref[base + 3 * job + 1] = source
                job_ref[base + 3 * job + 2] = list_ref[slots + k] - shard * col_blocks
                size_ref[shift] = job + 1

            at = jnp.clip(block, 0, row_blocks - 1)
            return jnp.where(wanted, jnp.maximum(count, seen[at] + 1), count)

        lax.fori_loop(0, list_ref[2 * slots], step, first)


def make_jobs(shards, owners, row_blocks, col_blocks, slot_list, host):
    slots = (slot_list.shape[0] - 1) // 2
    return pl.pallas_call(
        functools.partial(jobs_kernel, shards, owners, row_blocks, col_blocks),
        out_shape=(
            jax.ShapeDtypeStruct((shards * slots * 3,), jnp.int32),
            jax.ShapeDtypeStruct((shards + 2,), jnp.int32),
        ),
        in_specs=[SCALARS] * 2,
        out_specs=(SCALARS,) * 2,
        scratch_shapes=[pltpu.SMEM((row_blocks,), jnp.int32)],
        cost_estimate=pl.CostEstimate(flops=0, bytes_accessed=1 << 20, transcendentals=0),
        name="jobs",
    )(slot_list, host)


def pack_kernel(shift, row_blocks, mixed, send_ref, act_ref, *rest):
    *out_refs, buf, in_sems, out_sems = rest[1:] if mixed else rest
    count = buf.shape[0]

    @pl.loop(0, count)
    def _(j):
        block = send_ref[(shift - 1) * (row_blocks + 1) + j]

        def fetch(source):
            pltpu.make_async_copy(source, buf.at[j], in_sems.at[j]).start()

        if mixed:
            pl.when(block < row_blocks)(lambda: fetch(column(act_ref, block)))
            pl.when(block >= row_blocks)(lambda: fetch(column(rest[0], block - row_blocks)))
        else:
            fetch(column(act_ref, block))

    def each_out(act):
        first = 0
        for out_ref in out_refs:

            @pl.loop(0, out_ref.shape[0])
            def _(j):
                at = first + j
                act(at, pltpu.make_async_copy(buf.at[at], out_ref.at[j], out_sems.at[at]))

            first += out_ref.shape[0]

    def pass_on(at, copy):
        pltpu.make_async_copy(column(act_ref, 0), buf.at[at], in_sems.at[at]).wait()
        copy.start()

    each_out(pass_on)
    each_out(lambda _, copy: copy.wait())


def pack(shift, row_blocks, sizes, send, activations, *out_grad):
    tokens = activations.shape[0]
    count = sum(sizes)
    return pl.pallas_call(
        functools.partial(pack_kernel, shift, row_blocks, bool(out_grad)),
        out_shape=tuple(
            jax.ShapeDtypeStruct((size, tokens, BLK), activations.dtype) for size in sizes
        ),
        in_specs=[SCALARS] + [ANYWHERE] * (1 + len(out_grad)),
        out_specs=(ANYWHERE,) * len(sizes),
        scratch_shapes=[
            pltpu.VMEM((count, tokens, BLK), activations.dtype),
            pltpu.SemaphoreType.DMA((count,)),
            pltpu.SemaphoreType.DMA((count,)),
        ],
        compiler_params=pltpu.CompilerParams(
            vmem_limit_bytes=count * tokens * BLK * 2 + 2 * MIB
        ),
        cost_estimate=pl.CostEstimate(
            flops=0, bytes_accessed=count * tokens * BLK * 4, transcendentals=0
        ),
        name="pack",
    )(send, activations, *out_grad)


def multiply(rows, cols):
    return lax.dot_general(
        rows, cols, (((0,), (0,)), ((), ())), preferred_element_type=jnp.float32
    )


def column(ref, block):
    return ref.at[:, pl.ds(pl.multiple_of(block * BLK, BLK), BLK)]


def out_copy(stage, keep_ref, send_ref, sems, place, act, at=None):
    half = keep_ref.shape[0]
    at = place if at is None else at

    @pl.when(place < half)
    def _():
        act(pltpu.make_async_copy(stage.at[at], keep_ref.at[place], sems.at[place]))

    @pl.when(place >= half)
    def _():
        act(pltpu.make_async_copy(stage.at[at], send_ref.at[place - half], sems.at[place]))


def begin(copy):
    copy.start()


def finish(copy):
    copy.wait()


def here_kernel(shards, job_ref, size_ref, act_ref, grad_ref, *rest):
    _, _, keep_ref, send_ref, later_ref, row_buf, col_buf, stage, *sems = rest
    row_sems, col_sems, later_sems, out_sems = sems
    slots = later_ref.shape[0]
    depth = col_buf.shape[0]
    jobs = size_ref[0]
    out = functools.partial(out_copy, stage, keep_ref, send_ref, out_sems)

    def row_copy(job):
        at = lax.rem(job, depth)
        source = column(act_ref, job_ref[3 * job + 1])
        return pltpu.make_async_copy(source, row_buf.at[at], row_sems.at[at])

    def col_copy(job):
        at = lax.rem(job, depth)
        source = column(grad_ref, job_ref[3 * job + 2])
        return pltpu.make_async_copy(source, col_buf.at[at], col_sems.at[at])

    def each_later(act):
        before = jnp.int32(0)
        for shift in range(1, shards):

            @pl.loop(0, size_ref[shift])
            def _(job):
                source = column(grad_ref, job_ref[3 * (shift * slots + job) + 2])
                at = before + job
                act(pltpu.make_async_copy(source, later_ref.at[at], later_sems.at[at]))

            before = before + size_ref[shift]

    def start(job):
        row_copy(job).start()
        col_copy(job).start()

    pl.loop(0, jnp.minimum(depth, jobs))(start)
    each_later(begin)

    @pl.loop(0, jobs)
    def _(job):
        at = lax.rem(job, depth)
        place = job_ref[3 * job]
        row_copy(job).wait()
        col_copy(job).wait()
        stage[place] = multiply(row_buf[at], col_buf[at])
        out(place, begin)
        if depth < slots:
            pl.when(job + depth < jobs)(lambda: start(job + depth))

    each_later(finish)

    @pl.loop(0, jobs)
    def _(job):
        out(job_ref[3 * job], finish)


def products_here(shards, slots, jobs, sizes, activations, out_grad, partial):
    tokens = out_grad.shape[0]
    depth = min(slots, 8)
    half = jax.ShapeDtypeStruct((slots // 2, BLK, BLK), jnp.float32)
    room = 2 * depth * tokens * BLK * 2 + slots * BLK * BLK * 4 + 4 * MIB
    return pl.pallas_call(
        functools.partial(here_kernel, shards),
        out_shape=(half, half, jax.ShapeDtypeStruct((slots, tokens, BLK), out_grad.dtype)),
        in_specs=[SCALARS] * 2 + [ANYWHERE] * 4,
        out_specs=(ANYWHERE,) * 3,
        scratch_shapes=[
            pltpu.VMEM((depth, tokens, BLK), activations.dtype),
            pltpu.VMEM((depth, tokens, BLK), out_grad.dtype),
            pltpu.VMEM((slots, BLK, BLK), jnp.float32),
            pltpu.SemaphoreType.DMA((depth,)),
            pltpu.SemaphoreType.DMA((depth,)),
            pltpu.SemaphoreType.DMA((slots,)),
            pltpu.SemaphoreType.DMA((slots,)),
        ],
        input_output_aliases={4: 0, 5: 1},
        compiler_params=pltpu.CompilerParams(vmem_limit_bytes=room),
        cost_estimate=pl.CostEstimate(
            flops=slots * tokens * BLK * BLK,
            bytes_accessed=slots * tokens * BLK * 4,
            transcendentals=0,
        ),
        name="products_here",
    )(jobs, sizes, activations, out_grad, *partial)


def hosted_kernel(host_ref, act_ref, cols_ref, tiles_ref, row_buf, sems):
    def row_copy(n):
        source = column(act_ref, jnp.maximum(host_ref[2 + n], 0))
        return pltpu.make_async_copy(source, row_buf.at[n], sems.at[n])

    pl.loop(0, 2)(lambda n: row_copy(n).start())

    @pl.loop(0, 2)
    def _(n):
        row_copy(n).wait()
        tiles_ref[n] = multiply(row_buf[n], cols_ref[n])


def products_hosted(host, activations, cols):
    tokens = activations.shape[0]
    return pl.pallas_call(
        hosted_kernel,
        out_shape=jax.ShapeDtypeStruct((2, BLK, BLK), jnp.float32),
        in_specs=[SCALARS, ANYWHERE, IN_VMEM],
        out_specs=IN_VMEM,
        scratch_shapes=[
            pltpu.VMEM((2, tokens, BLK), activations.dtype),
            pltpu.SemaphoreType.DMA((2,)),
        ],
        compiler_params=pltpu.CompilerParams(vmem_limit_bytes=4 * MIB),
        cost_estimate=pl.CostEstimate(
            flops=4 * tokens * BLK * BLK, bytes_accessed=8 * tokens * BLK, transcendentals=0
        ),
        name="products_hosted",
    )(host, activations, cols)


def moved_kernel(shift, first, job_ref, size_ref, rows_ref, cols_ref, *rest):
    *back_refs, _, _, keep_ref, send_ref, stage, out_sems = rest
    slots = cols_ref.shape[0]
    out = functools.partial(out_copy, stage, keep_ref, send_ref, out_sems)
    before = jnp.int32(0)
    for earlier in range(1, shift):
        before = before + size_ref[earlier]

    def each_job(act):
        @pl.loop(0, size_ref[shift])
        def _(job):
            base = 3 * (shift * slots + job)
            block = job_ref[base + 1] - first

            @pl.when((block >= 0) & (block < rows_ref.shape[0]))
            def _():
                act(job, job_ref[base], block)

    def work(job, place, block):
        stage[place] = multiply(rows_ref[block], cols_ref[before + job])
        out(place, begin)

    def each_back(act):
        for back_ref in back_refs:

            @pl.loop(0, 2)
            def _(n):
                place = size_ref[size_ref.shape[0] - 2 + n]

                @pl.when(place >= 0)
                def _():
                    out_copy(back_ref, keep_ref, send_ref, out_sems, place, act, n)

    each_back(begin)
    each_job(work)
    each_job(lambda _, place, __: out(place, finish))
    each_back(finish)


def products_moved(shift, first, jobs, sizes, rows, cols, partial, back=()):
    slots, tokens = cols.shape[:2]
    half = jax.ShapeDtypeStruct((slots // 2, BLK, BLK), jnp.float32)
    room = (rows.shape[0] + slots) * tokens * BLK * 2 + slots * BLK * BLK * 4 + 4 * MIB
    return pl.pallas_call(
        functools.partial(moved_kernel, shift, first),
        out_shape=(half, half),
        in_specs=[SCALARS] * 2 + [IN_VMEM] * 2 + [ANYWHERE] * (2 + len(back)),
        out_specs=(ANYWHERE,) * 2,
        scratch_shapes=[
            pltpu.VMEM((slots, BLK, BLK), jnp.float32),
            pltpu.SemaphoreType.DMA((slots,)),
        ],
        input_output_aliases={4 + len(back): 0, 5 + len(back): 1},
        compiler_params=pltpu.CompilerParams(vmem_limit_bytes=room),
        cost_estimate=pl.CostEstimate(
            flops=slots * tokens * BLK * BLK,
            bytes_accessed=slots * tokens * BLK * 4,
            transcendentals=0,
        ),
        name="products_moved",
    )(jobs, sizes, rows, cols, *back, *partial)


def reduce_to_owner(owners, keep, send):
    lanes = (keep.shape[0] + send.shape[0]) // owners
    steps = owners.bit_length() - 1

    def swap(part, mask):
        return lax.ppermute(part, "dp", [(d, d ^ mask) for d in range(owners)])

    def halve(part, i):
        middle = part[0].shape[0] // 2
        arrived = swap(part[1], 1 << i)
        return [part[0][:middle] + arrived[:middle], part[0][middle:] + arrived[middle:]]

    if steps < 4:
        part = [keep, send]
        for i in range(steps - 1):
            part = halve(part, i)
        return part[0] + swap(part[1], 1 << (steps - 1))

    part = [keep, send]
    for i in range(steps - 4):
        part = halve(part, i)
    keep = part[0]
    came = swap(part[1], 1 << (steps - 4))

    def chunk(first):
        held = slice(first * lanes, (first + 2) * lanes)
        sent = slice((first + 4) * lanes, (first + 6) * lanes)
        return keep[held] + came[held], swap(keep[sent] + came[sent], 1 << (steps - 3))

    far_keep, far_came = chunk(2)
    near_keep, near_came = chunk(0)
    low, high = 1 << (steps - 2), 1 << (steps - 1)
    both_came = swap(far_keep[lanes:] + far_came[lanes:], low | high)
    low_came = swap(far_keep[:lanes] + far_came[:lanes], low)
    high_came = swap(near_keep[lanes:] + near_came[lanes:], high)
    return near_keep[:lanes] + near_came[:lanes] + both_came + low_came + high_came


def on_device(shards, owners, activations, out_grad, tile_list, tile_count):
    slots = tile_list.shape[1]
    row_blocks = activations.shape[1] // BLK
    col_blocks = out_grad.shape[1] // BLK

    slot_list = jnp.concatenate([tile_list[0, :, 0], tile_list[0, :, 1], tile_count])
    routes = [[(i, (i + s) % shards) for i in range(shards)] for s in range(shards)]
    lists = [slot_list] + [lax.ppermute(slot_list, "mp", routes[s]) for s in range(1, shards)]
    limit = min(row_blocks, slots)
    sizes = [n for n in (3, 4, 5, 6, 7, 8, 9, 10) if n < limit] + [limit]
    hosted_sizes = [n for n in (3, 4, 5, 6, 7, 8) if shards == 2 and n < limit]
    branch, send, host = make_plan(shards, row_blocks, col_blocks, sizes, hosted_sizes, lists)
    kinds = [(n, False) for n in sizes] + [(n, True) for n in hosted_sizes]

    carried = ()
    for shift in range(1, shards):

        def move(count, hosted, send, host, slot_list, carried, activations, out_grad):
            cut = [count - 1, 1]
            mixed = [out_grad] if hosted else []
            packed = pack(shift, row_blocks, cut, send, activations, *mixed)
            arrived = [lax.ppermute(part, "mp", routes[shift]) for part in packed]
            jobs, amounts = make_jobs(shards, owners, row_blocks, col_blocks, slot_list, host)
            if shift == 1:
                blank = jnp.zeros((slots // 2, BLK, BLK), jnp.float32)
                blank = lax.optimization_barrier((blank, blank))
                *partial, later = products_here(
                    shards, slots, jobs, amounts, activations, out_grad, blank
                )
            else:
                *partial, later = carried
            back = []
            if hosted:
                host, partial = lax.optimization_barrier((host, partial))
                tiles = products_hosted(host, activations, arrived[0])
                tiles, partial = lax.optimization_barrier((tiles, partial))
                back = [lax.ppermute(tiles, "mp", routes[shift])]
            for n, rows in enumerate(arrived):
                last = n + 1 == len(arrived)
                partial = products_moved(
                    shift, sum(cut[:n]), jobs, amounts, rows, later, partial, back if last else ()
                )
            if shift + 1 < shards:
                return *partial, later
            return reduce_to_owner(owners, *partial)[None]

        carried = lax.switch(
            branch[shift - 1],
            [functools.partial(move, count, hosted) for count, hosted in kinds],
            send,
            host,
            slot_list,
            carried,
            activations,
            out_grad,
        )
    return carried


def solution(mesh):
    placed = (P("dp", "mp"), P("dp", "mp"), P("mp", None, None), P("mp"))
    return jax.shard_map(
        functools.partial(on_device, mesh.shape["mp"], mesh.shape["dp"]),
        mesh=mesh,
        in_specs=placed,
        out_specs=P("mp", "dp", None, None),
        check_vma=False,
    )
```
